128 devices in a mesh: wide: 32 (over x, z, core), narrow: 4 (over y).
Axes of the slice: x: 4, y: 4, z: 4, core: 2. Of those that a mesh axis runs over, the one named last changes fastest.
Arguments:
- water_depth: float32 [8, 8, 163840], P(None, None, ('wide', 'narrow')), may hold values from 2 to 3
- momentum: float32 [2, 8, 8, 163840], P(None, None, None, ('wide', 'narrow')), may hold values from -3 to 3
- bathymetry: float32 [8, 8, 163840], P(None, None, ('wide', 'narrow')), may hold values from -0.5 to 0.5
- levels: int32 [163840], P(('wide', 'narrow')), may hold values from 0 to 1, as said below
- face_kind: int32 [4, 163840], P(None, ('wide', 'narrow')), may hold values from 0 to 3, as said below
- send_face: int32 [18432], P(('wide', 'narrow')), may hold values from 0 to 5119, as said below
- trace_src: int32 [4, 163840], P(None, ('wide', 'narrow')), may hold values from 0 to 5263, as said below
- return_face: int32 [12288], P(('wide', 'narrow')), may hold values from 0 to 5119, as said below
- mortar_src: int32 [2, 4, 163840], P(None, None, ('wide', 'narrow')), may hold values from 0 to 5215, as said below
Outputs:
- new_depth: float32 [8, 8, 163840], P(None, None, ('wide', 'narrow'))
- new_momentum: float32 [2, 8, 8, 163840], P(None, None, None, ('wide', 'narrow'))
The draws below stay inside these ranges and needn't reach their ends.
Inputs may be any that keep to these rules, and one draw needn't show every extreme that they name: `levels`: the mesh is a periodic forest of 32 x 8 trees of 16 x 16 blocks; the device at wide index w and narrow index n holds trees (w, 2n) and (w, 2n + 1) in that order; a block is one element of level 0 or four of level 1; elements of a tree in Morton order of blocks, children in Morton order. `face_kind`: 0: conforming neighbour; 1 or 2: a level 1 face whose neighbour is a level 0 face, touching its lower or upper half; 3: a level 0 face met by two level 1 faces. `send_face`: per device 144 slots in four blocks as in the reference program; a slot lists a local face id whose trace the neighbour needs; unused slots hold 0. Every block is full on some device in every draw. `trace_src`: for faces of kinds 0 to 2; 0 on faces of kind 3. `return_face`: per device 96 slots in four blocks as in the reference program; a slot lists a local face id of kind 1 or 2 whose neighbour owns the coarse face; unused slots hold 0. Every block is full on some device in every draw. `mortar_src`: lower and upper half for faces of kind 3, into [projected, returned]; 0 elsewhere.
All inputs are finite; a program needn't handle non-finite values.
Results may differ from the reference program's by a relative error of at most 0.0003.
Values sent between devices are 32-bit elements; how exact they have to be, the bound alone decides.
No kernel may reach another device: no remote copies, remote signals or barrier semaphores. Data moves between devices by JAX's collectives and lax.ppermute only.
A program may use at most 64 MiB of HBM per device.

```python
import jax
import jax.numpy as jnp
import numpy as np
from jax import lax

NODES = 8
TREE_SIDE = 16
PER_TREE = 640
E_DEV = 1280
ELEMENTS = 163840
CAP_X = 48
CAP_Y = 24
RET_X = 32
RET_Y = 16
SEND_DEV = 144
RET_DEV = 96
TREES_X = 32
TREES_Y = 8
N_WIDE = 32
N_NARROW = 4
DEVICES = 128


def morton_split(index_values, low_bits):
    coord_x = np.zeros(index_values.shape, np.int64)
    coord_y = np.zeros(index_values.shape, np.int64)
    for bit_pos in range(low_bits):
        coord_x = coord_x | (index_values >> 2 * bit_pos & 1) << bit_pos
        coord_y = coord_y | (index_values >> 2 * bit_pos + 1 & 1) << bit_pos
    coord_x = coord_x | index_values >> 2 * low_bits << low_bits
    return (coord_x, coord_y)


def rank_in_group(sort_keys, group_width):
    order_idx = jnp.argsort(sort_keys, stable=True)
    sorted_keys = sort_keys[order_idx]
    groups = sorted_keys // group_width
    positions = jnp.arange(sort_keys.shape[0], dtype=jnp.int32)
    starts = jnp.concatenate([jnp.ones((1,), jnp.int32), (groups[1:] != groups[:-1]).astype(jnp.int32)])
    first_pos = lax.cummax(positions * starts, axis=0)
    return jnp.zeros_like(sort_keys).at[order_idx].set(positions - first_pos)


def half_bits(key, count, forced_one, forced_zero):
    positions = jnp.arange(TREE_SIDE, dtype=jnp.int32)[None]
    scores = jax.random.randint(key, (count, TREE_SIDE), 0, 4096) * TREE_SIDE + positions
    scores = scores + jnp.asarray(forced_one, jnp.int32) * (4096 * TREE_SIDE)
    scores = jnp.where(jnp.asarray(forced_zero, jnp.int32) > 0, -1, scores)
    chosen = lax.top_k(scores, TREE_SIDE // 2)[1]
    row_ids = jnp.arange(count, dtype=jnp.int32)[:, None]
    return jnp.zeros((count, TREE_SIDE), jnp.int32).at[row_ids, chosen].set(1)


def mesh_tables(key):
    tree_side = TREE_SIDE
    block_total = tree_side * tree_side
    tree_total = TREES_X * TREES_Y
    per_tree = PER_TREE
    per_device = E_DEV
    block_x, block_y = morton_split(np.arange(block_total), tree_side.bit_length() - 1)
    block_at = np.zeros((tree_side, tree_side), np.int64)
    block_at[block_x, block_y] = np.arange(block_total)
    one_x = np.zeros((TREES_X, tree_side), np.int64)
    zero_x = np.zeros((TREES_X, tree_side), np.int64)
    zero_x[0, tree_side - 1] = 1
    one_x[1, 0] = 1
    one_x[1, tree_side - 1] = 1
    one_x[2 % TREES_X, 0] = 1
    one_y = np.zeros((TREES_Y, tree_side), np.int64)
    zero_y = np.zeros((TREES_Y, tree_side), np.int64)
    zero_y[1, tree_side - 1] = 1
    one_y[2, 0] = 1
    one_y[3, tree_side - 1] = 1
    one_y[4 % TREES_Y, 0] = 1
    zero_y[TREES_Y - 3, tree_side - 1] = 1
    one_y[TREES_Y - 2, 0] = 1
    zero_y[TREES_Y - 1, tree_side - 1] = 1
    one_y[0, 0] = 1
    column_key, row_key = jax.random.split(key)
    bits_x = half_bits(column_key, TREES_X, one_x, zero_x).reshape(-1)
    bits_y = half_bits(row_key, TREES_Y, one_y, zero_y).reshape(-1)
    tree_ids = np.arange(tree_total)
    index_x = (tree_ids // TREES_Y)[:, None] * tree_side + block_x[None]
    index_y = (tree_ids % TREES_Y)[:, None] * tree_side + block_y[None]
    refined = (bits_x[index_x] != bits_y[index_y]).astype(jnp.int32)
    block_sizes = 1 + 3 * refined
    starts_at = jnp.cumsum(block_sizes, axis=1) - block_sizes
    grid_w = 2 * tree_side * TREES_X
    grid_h = 2 * tree_side * TREES_Y
    cell_x = np.arange(grid_w)[:, None] + np.zeros((1, grid_h), np.int64)
    cell_y = np.zeros((grid_w, 1), np.int64) + np.arange(grid_h)[None, :]
    cell_tree = cell_x // (2 * tree_side) * TREES_Y + cell_y // (2 * tree_side)
    cell_block = block_at[cell_x % (2 * tree_side) // 2, cell_y % (2 * tree_side) // 2]
    cell_child = cell_x % 2 + 2 * (cell_y % 2)
    cell_ref = refined[cell_tree, cell_block]
    owner = jnp.asarray(cell_tree * per_tree, jnp.int32) + starts_at[cell_tree, cell_block] + cell_ref * jnp.asarray(cell_child, jnp.int32)
    flat_owner = owner.reshape(-1)
    level_of = jnp.zeros((ELEMENTS,), jnp.int32).at[flat_owner].set(cell_ref.reshape(-1))
    anchor_x = jnp.zeros((ELEMENTS,), jnp.int32).at[flat_owner].set((jnp.asarray(cell_x, jnp.int32) - jnp.asarray(cell_x % 2, jnp.int32) * (1 - cell_ref)).reshape(-1))
    anchor_y = jnp.zeros((ELEMENTS,), jnp.int32).at[flat_owner].set((jnp.asarray(cell_y, jnp.int32) - jnp.asarray(cell_y % 2, jnp.int32) * (1 - cell_ref)).reshape(-1))
    extent = 2 - level_of
    probe_first = [(anchor_x - 1, anchor_y), (anchor_x + extent, anchor_y), (anchor_x, anchor_y - 1), (anchor_x, anchor_y + extent)]
    probe_second = [(anchor_x - 1, anchor_y + extent - 1), (anchor_x + extent, anchor_y + extent - 1), (anchor_x + extent - 1, anchor_y - 1), (anchor_x + extent - 1, anchor_y + extent)]
    near_first = jnp.stack([owner[probe[0] % grid_w, probe[1] % grid_h] for probe in probe_first])
    near_second = jnp.stack([owner[probe[0] % grid_w, probe[1] % grid_h] for probe in probe_second])
    tangent_own = jnp.stack([anchor_y, anchor_y, anchor_x, anchor_x])
    tangent_other = jnp.stack([anchor_y[near_first[0]], anchor_y[near_first[1]], anchor_x[near_first[2]], anchor_x[near_first[3]]])
    period = jnp.asarray(np.array([grid_h, grid_h, grid_w, grid_w]), jnp.int32)[:, None]
    half_index = (tangent_own - tangent_other) % period
    coarse_kind = jnp.where(near_first != near_second, 3, 0)
    fine_kind = jnp.where(level_of[near_first] == 0, 1 + half_index, 0)
    kinds = jnp.where(level_of[None] == 0, coarse_kind, fine_kind).astype(jnp.int32)
    element_ids = jnp.arange(ELEMENTS, dtype=jnp.int32)[None]
    face_ids = jnp.arange(4, dtype=jnp.int32)[:, None]
    home_dev = element_ids // per_device
    local_id = face_ids * per_device + element_ids % per_device
    opposite = face_ids + 1 - 2 * (face_ids % 2)
    source_dev = near_first // per_device
    target_local = opposite * per_device + near_first % per_device
    remote = source_dev != home_dev
    trace_offs = jnp.asarray(np.array([0, CAP_X, 2 * CAP_X, 2 * CAP_X + CAP_Y]), jnp.int32)[:, None]
    trace_back = jnp.asarray(np.array([CAP_X, 0, 2 * CAP_X + CAP_Y, 2 * CAP_X]), jnp.int32)[:, None]
    ret_offs = jnp.asarray(np.array([0, RET_X, 2 * RET_X, 2 * RET_X + RET_Y]), jnp.int32)[:, None]
    ret_back = jnp.asarray(np.array([RET_X, 0, 2 * RET_X + RET_Y, 2 * RET_X]), jnp.int32)[:, None]
    needs_trace = (kinds != 3) & remote
    flat_index = face_ids * ELEMENTS + element_ids
    span_one = 4 * per_device
    sort_keys = jnp.where(needs_trace, (home_dev * 4 + face_ids) * span_one + local_id, DEVICES * 4 * span_one + flat_index)
    slot_rank = rank_in_group(sort_keys.reshape(-1), span_one).reshape(4, ELEMENTS)
    trace_table = jnp.where(kinds == 3, 0, jnp.where(remote, span_one + trace_offs + slot_rank, target_local))
    send_slot = jnp.where(needs_trace, source_dev * SEND_DEV + trace_back + slot_rank, DEVICES * SEND_DEV)
    send_table = jnp.zeros((DEVICES * SEND_DEV,), jnp.int32).at[send_slot.reshape(-1)].set(target_local.reshape(-1), mode='drop')
    near_both = jnp.stack([near_first, near_second])
    half_ids = jnp.arange(2, dtype=jnp.int32)[:, None, None]
    target_two = opposite[None] * per_device + near_both % per_device
    source_two = near_both // per_device
    is_mortar = ((kinds == 3) & remote)[None]
    keys_two = jnp.where(is_mortar, ((home_dev * 4 + face_ids) * (2 * span_one) + 2 * local_id)[None] + half_ids, DEVICES * 4 * 2 * span_one + half_ids * (4 * ELEMENTS) + flat_index[None])
    rank_two = rank_in_group(keys_two.reshape(-1), 2 * span_one).reshape(2, 4, ELEMENTS)
    mortar_table = jnp.where((kinds == 3)[None], jnp.where(remote[None], span_one + ret_offs[None] + rank_two, target_two), 0)
    return_slot = jnp.where(is_mortar, source_two * RET_DEV + ret_back[None] + rank_two, DEVICES * RET_DEV)
    return_table = jnp.zeros((DEVICES * RET_DEV,), jnp.int32).at[return_slot.reshape(-1)].set(target_two.reshape(-1), mode='drop')
    return (level_of, kinds, send_table, trace_table.astype(jnp.int32), return_table, mortar_table.astype(jnp.int32))


def draw_levels(key, part):
    return mesh_tables(key)[0]


def draw_face_kind(key, part):
    return mesh_tables(key)[1]


def draw_send_face(key, part):
    return mesh_tables(key)[2]


def draw_trace_src(key, part):
    return mesh_tables(key)[3]


def draw_return_face(key, part):
    return mesh_tables(key)[4]


def draw_mortar_src(key, part):
    return mesh_tables(key)[5]


def block_levels(own_key, shape, pieces, smallest, high):
    def one(position, parts):
        steps = jax.random.uniform(jax.random.fold_in(jax.random.fold_in(own_key, 6), position), (parts,), jnp.float32, smallest / len(pieces), high / len(pieces))
        return jnp.repeat(jnp.exp(steps), shape[position] // parts).reshape((-1,) + (1,) * (len(shape) - position - 1))

    gain = one(*pieces[0])
    for cut in pieces[1:]:
        gain = gain * one(*cut)
    return gain


def bell_draw(key, dims, scale, bound, pieces=(), held_as=jnp.bfloat16):
    result = jax.random.normal(key, dims, jnp.float32) * scale
    if len(pieces) > 0:
        result = block_levels(key, dims, pieces, -0.22, 0.18) * result
    return jnp.clip(result, min=-bound, max=bound).astype(held_as)


def setup_inputs(seed: int = 0) -> dict:
    splits = jax.random.split(jax.random.key(seed), 10)
    return {
        "water_depth": jnp.clip(2.0 + 1.0 * jax.random.uniform(splits[0], (NODES, NODES, ELEMENTS), jnp.float32) ** block_levels(splits[0], (NODES, NODES, ELEMENTS), ((2, 128),), -0.2, 0.2), 2.0, 3.0),
        "momentum": bell_draw(splits[1], (2, NODES, NODES, ELEMENTS), 0.6, 3.0, ((3, 128),), jnp.float32),
        "bathymetry": jnp.clip(jax.random.uniform(splits[2], (NODES, NODES, ELEMENTS), jnp.float32, -0.5, 0.5) * block_levels(splits[2], (NODES, NODES, ELEMENTS), ((2, 128),), -0.4, 0.0), -0.5, 0.5),
        "levels": draw_levels(jax.random.fold_in(splits[9], 71), 0),
        "face_kind": draw_face_kind(jax.random.fold_in(splits[9], 71), 0),
        "send_face": draw_send_face(jax.random.fold_in(splits[9], 71), 0),
        "trace_src": draw_trace_src(jax.random.fold_in(splits[9], 71), 0),
        "return_face": draw_return_face(jax.random.fold_in(splits[9], 71), 0),
        "mortar_src": draw_mortar_src(jax.random.fold_in(splits[9], 71), 0),
    }


gravity = 1.0
time_step = 0.005

def legendre_pair(points, degree):
    before = np.ones(points.shape)
    current = points * 1.0
    for order in range(2, degree + 1):
        following = ((2.0 * order - 1.0) * points * current - (order - 1.0) * before) / order
        before = current
        current = following
    return (current, before)

def lgl_tables():
    degree = 7
    point_count = degree + 1
    points = -np.cos(np.pi * np.arange(point_count) / degree)
    for sweep in range(100):
        top_value, below_value = legendre_pair(points, degree)
        points = points - (points * top_value - below_value) / (point_count * top_value)
    points[0] = -1.0
    points[-1] = 1.0
    values = legendre_pair(points, degree)[0]
    weights = 2.0 / (degree * point_count * values * values)
    derivative = np.zeros((point_count, point_count))
    for row_id in range(point_count):
        for col_id in range(point_count):
            if row_id != col_id:
                derivative[row_id, col_id] = values[row_id] / (values[col_id] * (points[row_id] - points[col_id]))
    derivative[0, 0] = -degree * point_count / 4.0
    derivative[-1, -1] = degree * point_count / 4.0

    def lagrange(targets):
        lagrange_table = np.ones((point_count, point_count))
        for col_id in range(point_count):
            for other_id in range(point_count):
                if other_id != col_id:
                    lagrange_table[:, col_id] = lagrange_table[:, col_id] * (targets - points[other_id]) / (points[col_id] - points[other_id])
        return lagrange_table
    interp_lower = lagrange((points - 1.0) / 2.0)
    interp_upper = lagrange((points + 1.0) / 2.0)
    proj_lower = 0.5 * interp_lower.T * weights[None, :] / weights[:, None]
    proj_upper = 0.5 * interp_upper.T * weights[None, :] / weights[:, None]
    lift_end = 1.0 / weights[0]
    return (lift_end, jnp.asarray(derivative, jnp.float32), jnp.asarray(interp_lower, jnp.float32), jnp.asarray(interp_upper, jnp.float32), jnp.asarray(proj_lower, jnp.float32), jnp.asarray(proj_upper, jnp.float32))

def point_pair(height_l, normal_l, tangent_l, height_r, normal_r, tangent_r):
    mean_h = 0.5 * (height_l + height_r)
    mean_n = 0.5 * (normal_l + normal_r)
    mean_t = 0.5 * (tangent_l + tangent_r)
    square_h = 0.5 * (height_l * height_l + height_r * height_r)
    return (mean_h * mean_n, mean_h * mean_n * mean_n + 0.5 * gravity * square_h, mean_h * mean_n * mean_t)

def face_traces(height, mom_x, mom_y, bed):
    stacked = jnp.stack([height, mom_x, mom_y, bed])
    sides = jnp.stack([stacked[:, 0], stacked[:, -1], stacked[:, :, 0], stacked[:, :, -1]], axis=2)
    return sides.reshape(32, -1)

def face_flux(own, other, face_id):
    normal_sign = -1.0 if face_id % 2 == 0 else 1.0
    normal_id = 1 if face_id < 2 else 2
    tangent_id = 3 - normal_id
    vel_n_own = own[normal_id] / own[0]
    vel_t_own = own[tangent_id] / own[0]
    vel_n_other = other[normal_id] / other[0]
    vel_t_other = other[tangent_id] / other[0]
    flux_mass, flux_normal, flux_tangent = point_pair(own[0], vel_n_own, vel_t_own, other[0], vel_n_other, vel_t_other)
    speed = jnp.maximum(jnp.abs(vel_n_own) + jnp.sqrt(gravity * own[0]), jnp.abs(vel_n_other) + jnp.sqrt(gravity * other[0]))
    num_h = normal_sign * flux_mass - 0.5 * speed * (other[0] + other[3] - (own[0] + own[3]))
    num_n = normal_sign * flux_normal - 0.5 * speed * (other[normal_id] - own[normal_id])
    num_t = normal_sign * flux_tangent - 0.5 * speed * (other[tangent_id] - own[tangent_id])
    phys_h = normal_sign * own[normal_id]
    phys_n = normal_sign * (own[normal_id] * vel_n_own + 0.5 * gravity * own[0] * own[0])
    phys_t = normal_sign * own[normal_id] * vel_t_own
    if normal_id == 1:
        return (jnp.stack([num_h, num_n, num_t]), jnp.stack([phys_h, phys_n, phys_t]))
    return (jnp.stack([num_h, num_t, num_n]), jnp.stack([phys_h, phys_t, phys_n]))

def surface_fluxes(local, received, kinds, trace_index, tables):
    element_count = kinds.shape[1]
    interp_lower, interp_upper, proj_lower, proj_upper = (tables[2], tables[3], tables[4], tables[5])
    highest = lax.Precision.HIGHEST
    trace_pool = jnp.concatenate([local, received], axis=1)
    gathered = trace_pool[:, trace_index.reshape(-1)].reshape(4, 8, 4, element_count)
    own_all = local.reshape(4, 8, 4, element_count)
    from_lower = jnp.einsum('ab,cbfe->cafe', interp_lower, gathered, precision=highest)
    from_upper = jnp.einsum('ab,cbfe->cafe', interp_upper, gathered, precision=highest)
    selector = kinds[None, None]
    other_all = jnp.where(selector == 1, from_lower, jnp.where(selector == 2, from_upper, gathered))
    numeric_list = []
    physical_list = []
    for face_id in range(4):
        numeric_face, physical_face = face_flux(own_all[:, :, face_id], other_all[:, :, face_id], face_id)
        numeric_list.append(numeric_face)
        physical_list.append(physical_face)
    numeric = jnp.stack(numeric_list, axis=2)
    physical = jnp.stack(physical_list, axis=2)
    onto_lower = jnp.einsum('ab,cbfe->cafe', proj_lower, numeric, precision=highest)
    onto_upper = jnp.einsum('ab,cbfe->cafe', proj_upper, numeric, precision=highest)
    projected = jnp.where(selector == 1, onto_lower, onto_upper)
    return (numeric, physical, projected.reshape(24, -1))

def volume_rates(height, mom_x, mom_y, bed, derivative):
    highest = lax.Precision.HIGHEST
    vel_x = mom_x / height
    vel_y = mom_y / height
    pair_x = point_pair(height[:, None], vel_x[:, None], vel_y[:, None], height[None], vel_x[None], vel_y[None])
    factor_x = 2.0 * derivative[:, :, None, None]
    rate_h = -lax.optimization_barrier(jnp.sum(factor_x * pair_x[0], axis=1))
    rate_x = -lax.optimization_barrier(jnp.sum(factor_x * pair_x[1], axis=1))
    rate_y = -lax.optimization_barrier(jnp.sum(factor_x * pair_x[2], axis=1))
    pair_y = point_pair(height[:, :, None], vel_y[:, :, None], vel_x[:, :, None], height[:, None], vel_y[:, None], vel_x[:, None])
    factor_y = 2.0 * derivative[None, :, :, None]
    rate_h = rate_h - lax.optimization_barrier(jnp.sum(factor_y * pair_y[0], axis=2))
    rate_y = rate_y - lax.optimization_barrier(jnp.sum(factor_y * pair_y[1], axis=2))
    rate_x = rate_x - lax.optimization_barrier(jnp.sum(factor_y * pair_y[2], axis=2))
    slope_x = jnp.einsum('ik,kje->ije', derivative, bed, precision=highest)
    slope_y = jnp.einsum('jk,ike->ije', derivative, bed, precision=highest)
    rate_x = rate_x - gravity * height * slope_x
    rate_y = rate_y - gravity * height * slope_y
    return jnp.stack([rate_h, rate_x, rate_y])

def mortar_from_pool(pool_two, mortar_index, element_count):
    return (pool_two[:, mortar_index[0].reshape(-1)] + pool_two[:, mortar_index[1].reshape(-1)]).reshape(3, 8, 4, element_count)

def finish_section(height, momentum, bed, levels, numeric, physical, kinds, mortar, tables):
    lift_end, derivative = (tables[0], tables[1])
    numeric = jnp.where(kinds[None, None] == 3, -mortar, numeric)
    flux_jump = numeric - physical
    metric = (1 + levels).astype(jnp.float32)
    rate_all = volume_rates(height, momentum[0], momentum[1], bed, derivative) * metric
    lifted = lift_end * metric * flux_jump
    rate_all = rate_all.at[:, 0].add(-lifted[:, :, 0])
    rate_all = rate_all.at[:, -1].add(-lifted[:, :, 1])
    rate_all = rate_all.at[:, :, 0].add(-lifted[:, :, 2])
    rate_all = rate_all.at[:, :, -1].add(-lifted[:, :, 3])
    new_height = height + time_step * rate_all[0]
    new_moment = momentum + time_step * rate_all[1:]
    return (new_height, new_moment)

def by_device(array):
    lead_shape = array.shape[:-1]
    return jnp.moveaxis(array.reshape(lead_shape + (DEVICES, -1)), -2, 0)

def from_devices(array):
    moved = jnp.moveaxis(array, 0, -2)
    return moved.reshape(moved.shape[:-2] + (-1,))

def neighbour_ids(target):
    wide_id = target // N_NARROW
    narrow_id = target % N_NARROW
    wide_down = (wide_id + N_WIDE - 1) % N_WIDE * N_NARROW + narrow_id
    wide_up = (wide_id + 1) % N_WIDE * N_NARROW + narrow_id
    narrow_down = wide_id * N_NARROW + (narrow_id + N_NARROW - 1) % N_NARROW
    narrow_up = wide_id * N_NARROW + (narrow_id + 1) % N_NARROW
    return (wide_down, wide_up, narrow_down, narrow_up)

def collect(buffers, target, cap_x, cap_y):
    wide_down, wide_up, narrow_down, narrow_up = neighbour_ids(target)
    return jnp.concatenate([buffers[wide_down][:, cap_x:2 * cap_x], buffers[wide_up][:, :cap_x], buffers[narrow_down][:, 2 * cap_x + cap_y:], buffers[narrow_up][:, 2 * cap_x:2 * cap_x + cap_y]], axis=1)

def pick_columns(table, columns):
    return table[:, columns]

def reference(water_depth, momentum, bathymetry, levels, face_kind, send_face, trace_src, return_face, mortar_src):
    tables = lgl_tables()
    depth_dev = by_device(water_depth)
    moment_dev = by_device(momentum)
    bed_dev = by_device(bathymetry)
    level_dev = by_device(levels)
    kind_dev = by_device(face_kind)
    trace_dev = by_device(trace_src)
    mortar_dev = by_device(mortar_src)
    local_all = jax.vmap(face_traces)(depth_dev, moment_dev[:, 0], moment_dev[:, 1], bed_dev)
    send_table = send_face.reshape(DEVICES, SEND_DEV)
    return_table = return_face.reshape(DEVICES, RET_DEV)
    outgoing_all = jax.vmap(pick_columns)(local_all, send_table)
    device_ids = jnp.arange(DEVICES, dtype=jnp.int32)

    def first_pass(target):
        received = collect(outgoing_all, target, CAP_X, CAP_Y)
        projected = surface_fluxes(local_all[target], received, kind_dev[target], trace_dev[target], tables)[2]
        return projected[:, return_table[target]]
    returning_all = lax.map(first_pass, device_ids)

    def second_pass(target):
        received = collect(outgoing_all, target, CAP_X, CAP_Y)
        numeric, physical, projected = surface_fluxes(local_all[target], received, kind_dev[target], trace_dev[target], tables)
        returned = collect(returning_all, target, RET_X, RET_Y)
        pool_two = jnp.concatenate([projected, returned], axis=1)
        mortar = mortar_from_pool(pool_two, mortar_dev[target], E_DEV)
        return finish_section(depth_dev[target], moment_dev[target], bed_dev[target], level_dev[target], numeric, physical, kind_dev[target], mortar, tables)
    new_height, new_moment = lax.map(second_pass, device_ids)
    return (from_devices(new_height), from_devices(new_moment))
```

```python
import jax
import jax.numpy as jnp
import numpy as np
from jax import lax
from jax.experimental import pallas as pl
from jax.experimental.pallas import tpu as pltpu
from jax.sharding import PartitionSpec as P

NODES = 8
ELEMS = 1280
LANES = 128
BLOCKS = ELEMS // LANES
TREE_BLOCKS = BLOCKS // 2
FACES = 4
STATE, TRACE, MOVED = 256, 128, 192
LOCAL = FACES * ELEMS
STEP = 0.005
F32 = jnp.float32
I32 = jnp.int32

SEND_AT = (0, 48, 96, 120)
SEND_CAP = (48, 48, 24, 24)
BACK_AT = (48, 96, 64, 80)
BACK_CAP = (32, 32, 16, 16)
RECV_OFF = (0, 48, 96, 120)
RECV_LANE = (48, 0, 120, 96)
RETN_OFF = (0, 32, 64, 80)
RETN_LANE = (96, 48, 80, 64)


def tables():
    degree = NODES - 1

    def legendre(points):
        before, current = np.ones(points.shape), points * 1.0
        for order in range(2, degree + 1):
            before, current = (
                current,
                ((2.0 * order - 1.0) * points * current - (order - 1.0) * before) / order,
            )
        return current, before

    points = -np.cos(np.pi * np.arange(NODES) / degree)
    for _ in range(100):
        top, below = legendre(points)
        points = points - (points * top - below) / (NODES * top)
    points[0], points[-1] = -1.0, 1.0
    values = legendre(points)[0]
    weights = 2.0 / (degree * NODES * values * values)
    deriv = np.zeros((NODES, NODES))
    for i in range(NODES):
        for k in range(NODES):
            if i != k:
                deriv[i, k] = values[i] / (values[k] * (points[i] - points[k]))

    def lagrange(targets):
        table = np.ones((NODES, NODES))
        for k in range(NODES):
            for o in range(NODES):
                if o != k:
                    table[:, k] = table[:, k] * (targets - points[o]) / (points[k] - points[o])
        return table

    low, high = lagrange((points - 1.0) / 2.0), lagrange((points + 1.0) / 2.0)
    proj_low = 0.5 * low.T * weights[None, :] / weights[:, None]
    proj_high = 0.5 * high.T * weights[None, :] / weights[:, None]
    return weights, deriv, low, high, proj_low, proj_high


WEIGHTS, DERIV, INTERP_LOW, INTERP_HIGH, PROJ_LOW, PROJ_HIGH = tables()
SKEW = WEIGHTS[:, None] * DERIV
LIFT = 1.0 / WEIGHTS[0]


def column_tables():
    stack = np.stack([INTERP_LOW, INTERP_HIGH, PROJ_LOW, PROJ_HIGH]).transpose(0, 2, 1)
    return np.broadcast_to(stack.reshape(4 * NODES * NODES, 1), (4 * NODES * NODES, LANES)).astype(
        np.float32
    )


def face_rows(base, face):
    if face == 0:
        return pl.ds(base, 8)
    if face == 1:
        return pl.ds(base + 56, 8)
    if face == 2:
        return pl.ds(base, 8, stride=8)
    return pl.ds(base + 7, 8, stride=8)


def lanes_of(block):
    return pl.ds(pl.multiple_of(block * LANES, LANES), LANES)


def spread(row):
    return jnp.broadcast_to(row, (8, LANES))


def pick(source, lane):
    return jnp.take_along_axis(source, lane, axis=1, mode="promise_in_bounds")


def pack_kernel(depth, moment, bed, send, back, state, traces, wide_a, wide_b, narrow_a, narrow_b, sems):
    copies = []
    for block in range(BLOCKS):
        lanes = pl.ds(block * LANES, LANES)
        base = block * STATE
        for slot, (source, row, count) in enumerate(
            ((depth, 0, 64), (moment, 64, 128), (bed, 192, 64))
        ):
            copies.append(
                pltpu.make_async_copy(
                    source.at[:, lanes], state.at[pl.ds(base + row, count)], sems.at[slot, block]
                )
            )
    for copy in copies:
        copy.start()
    lane_id = lax.broadcasted_iota(I32, (8, LANES), 1)
    send_first = spread(send[:, 0:LANES])
    send_last = spread(send[:, LANES : 2 * LANES])
    back_row = spread(back[:, 0:LANES])
    backs = (
        pltpu.roll(back_row, 48, 1),
        pltpu.roll(back_row, 64, 1),
        back_row,
        back_row,
    )
    index = []
    for way in range(4):
        row = send_first
        if way == 3:
            row = jnp.where(lane_id < 64, send_last, send_first)
        inside = (lane_id >= BACK_AT[way]) & (lane_id < BACK_AT[way] + BACK_CAP[way])
        row = jnp.where(inside, backs[way], row)
        index.append(row - way * ELEMS)
    for copy in copies:
        copy.wait()
    for block in range(BLOCKS):
        for face in range(FACES):
            for comp in range(4):
                traces[pl.ds(block * TRACE + (face * 4 + comp) * 8, 8), :] = state[
                    face_rows(block * STATE + comp * 64, face), :
                ]
    out = []
    for way in range(4):
        lane = index[way] & (LANES - 1)
        place = index[way] >> 7
        found = []
        for comp in range(4):
            base = (way * 4 + comp) * 8
            total = jnp.zeros((8, LANES), F32)
            for block in range(BLOCKS):
                got = pick(traces[pl.ds(block * TRACE + base, 8), :], lane)
                total = jnp.where(place == block, got, total)
            found.append(total)
        out.append(found)
    wide_even = (lax.axis_index("wide") & 1) == 0
    narrow_even = (lax.axis_index("narrow") & 1) == 0
    for comp in range(4):
        rows = pl.ds(comp * 8, 8)
        wide_a[rows, :] = jnp.where(wide_even, out[1][comp], out[0][comp])
        wide_b[rows, :] = jnp.where(wide_even, out[0][comp], out[1][comp])
        narrow_a[rows, :] = jnp.where(narrow_even, out[3][comp], out[2][comp])
        narrow_b[rows, :] = jnp.where(narrow_even, out[2][comp], out[3][comp])


def line_terms(height, normal, tangent, bed):
    square = [2.0 * h * h for h in height]
    mass = [None] * 8
    along = [None] * 8
    cross = [None] * 8
    slope = [None] * 8

    def add(slot, i, value):
        slot[i] = value if slot[i] is None else slot[i] + value

    def sub(slot, i, value):
        slot[i] = -value if slot[i] is None else slot[i] - value

    for i in range(8):
        for k in range(i + 1, 8):
            q = float(SKEW[i, k])
            un = normal[i] + normal[k]
            ut = tangent[i] + tangent[k]
            first = (q * (height[i] + height[k])) * un
            second = first * un + q * (square[i] + square[k])
            third = first * ut
            bump = q * (bed[k] - bed[i])
            add(mass, i, first)
            sub(mass, k, first)
            add(along, i, second)
            sub(along, k, second)
            add(cross, i, third)
            sub(cross, k, third)
            add(slope, i, bump)
            add(slope, k, bump)
    out = []
    for i in range(8):
        scale = STEP / WEIGHTS[i]
        out.append(
            (
                float(0.5 * scale) * mass[i],
                float(0.25 * scale) * (along[i] + (4.0 * height[i]) * slope[i]),
                float(0.25 * scale) * cross[i],
            )
        )
    return out


def volume_kernel(state, levels, moved, scratch):
    def body(block, carry):
        lanes = lanes_of(block)
        metric = spread((levels[:, lanes] + 1).astype(F32))
        base = pl.multiple_of(block * STATE, STATE)
        into = pl.multiple_of(block * MOVED, MOVED)

        def load(comp, j, across):
            if across:
                return state[pl.ds(base + comp * 64 + j, 8, stride=8), :]
            return state[pl.ds(base + comp * 64 + j * 8, 8), :]

        for across in (True, False):
            height = [load(0, j, across) for j in range(8)]
            inverse = [1.0 / h for h in height]
            vel_x = [load(1, j, across) * inverse[j] for j in range(8)]
            vel_y = [load(2, j, across) * inverse[j] for j in range(8)]
            bed = [load(3, j, across) for j in range(8)]
            if across:
                terms = line_terms(height, vel_y, vel_x, bed)
                for j in range(8):
                    mass, along, cross = terms[j]
                    scratch[pl.ds(j, 8, stride=8), :] = mass
                    scratch[pl.ds(64 + j, 8, stride=8), :] = cross
                    scratch[pl.ds(128 + j, 8, stride=8), :] = along
            else:
                terms = line_terms(height, vel_x, vel_y, bed)
                for i in range(8):
                    mass, along, cross = terms[i]
                    for comp, value in enumerate((mass, along, cross)):
                        row = comp * 64 + i * 8
                        moved[pl.ds(into + row, 8), :] = state[pl.ds(base + row, 8), :] - metric * (
                            value + scratch[pl.ds(row, 8), :]
                        )
        return carry

    lax.fori_loop(0, BLOCKS, body, 0)


def apply(table, pieces):
    total = None
    for node in range(8):
        term = table[node] * spread(pieces[node : node + 1, :])
        total = term if total is None else total + term
    return total


def numeric_flux(left, right, sign):
    inv_l, inv_r = 1.0 / left[0], 1.0 / right[0]
    un_l, un_r = left[1] * inv_l, right[1] * inv_r
    ut_l, ut_r = left[2] * inv_l, right[2] * inv_r
    un = un_l + un_r
    ut = ut_l + ut_r
    speed = jnp.maximum(
        jnp.abs(un_l) + jnp.sqrt(left[0]), jnp.abs(un_r) + jnp.sqrt(right[0])
    )
    half = 0.5 * speed
    first = (0.25 * sign) * (left[0] + right[0]) * un
    second = 0.5 * (first * un) + (0.25 * sign) * (left[0] * left[0] + right[0] * right[0])
    third = 0.5 * (first * ut)
    return (
        first - half * ((right[0] + right[3]) - (left[0] + left[3])),
        second - half * (right[1] - left[1]),
        third - half * (right[2] - left[2]),
    )


def surface_kernel(
    moved, traces, got_wa, got_wb, got_na, got_nb, kinds, trace_src, mortar_src, levels, table_ref,
    new_depth, new_moment, result, sems
):
    wide_even = (lax.axis_index("wide") & 1) == 0
    narrow_even = (lax.axis_index("narrow") & 1) == 0

    def came(face, comp):
        rows = pl.ds(comp * 8, 8)
        if face == 0:
            return jnp.where(wide_even, got_wb[rows, :], got_wa[rows, :])
        if face == 1:
            return jnp.where(wide_even, got_wa[rows, :], got_wb[rows, :])
        if face == 2:
            return jnp.where(narrow_even, got_nb[rows, :], got_na[rows, :])
        return jnp.where(narrow_even, got_na[rows, :], got_nb[rows, :])

    def table(which, node):
        return table_ref[pl.ds((which * 8 + node) * 8, 8), :]

    def copies(block):
        lanes = lanes_of(block)
        row = pl.multiple_of(block * MOVED, MOVED)
        return (
            pltpu.make_async_copy(
                result.at[pl.ds(row, 64)], new_depth.at[:, lanes], sems.at[0, block]
            ),
            pltpu.make_async_copy(
                result.at[pl.ds(row + 64, 128)], new_moment.at[:, lanes], sems.at[1, block]
            ),
        )

    def body(block, carry):
        lanes = lanes_of(block)
        into = pl.multiple_of(block * MOVED, MOVED)
        held = pl.multiple_of(block * TRACE, TRACE)
        for row in range(24):
            rows = pl.ds(into + row * 8, 8)
            result[rows, :] = moved[rows, :]
        factor = spread((levels[:, lanes] + 1).astype(F32)) * float(LIFT * STEP)
        for face in range(FACES):
            opposite = face ^ 1
            kind = spread(kinds[face : face + 1, lanes])
            fine_low = spread(mortar_src[face : face + 1, lanes])
            fine_high = spread(mortar_src[4 + face : 5 + face, lanes])
            source = spread(trace_src[face : face + 1, lanes])
            coarse = kind == 3
            first = jnp.where(coarse, fine_low, source)
            back_shift = RETN_LANE[face] - RETN_OFF[face] - LOCAL
            shift = jnp.where(coarse, back_shift, RECV_LANE[face] - RECV_OFF[face] - LOCAL)
            first_far = first >= LOCAL
            high_far = fine_high >= LOCAL
            first = first + jnp.where(first_far, shift, -opposite * ELEMS)
            high = fine_high + jnp.where(high_far, back_shift, -opposite * ELEMS)
            first_place = jnp.where(first_far, BLOCKS, first >> 7)
            high_place = jnp.where(high_far, BLOCKS, high >> 7)
            first_lane = first & (LANES - 1)
            high_lane = high & (LANES - 1)
            near = []
            above = []
            for comp in range(4):
                base = (opposite * 4 + comp) * 8
                arrived = came(face, comp)
                one = pick(arrived, first_lane)
                two = pick(arrived, high_lane)
                for other in range(BLOCKS):
                    piece = traces[pl.ds(other * TRACE + base, 8), :]
                    one = jnp.where(first_place == other, pick(piece, first_lane), one)
                    two = jnp.where(high_place == other, pick(piece, high_lane), two)
                near.append(one)
                above.append(two)
            own = [traces[pl.ds(held + (face * 4 + comp) * 8, 8), :] for comp in range(4)]
            blend = [jnp.where(coarse, own[c], near[c]) for c in range(4)]
            low = [apply([table(0, n) for n in range(8)], b) for b in blend]
            high_of = [apply([table(1, n) for n in range(8)], b) for b in blend]
            left = [jnp.where(coarse, low[c], own[c]) for c in range(4)]
            right = [
                jnp.where(kind == 1, low[c], jnp.where(kind == 2, high_of[c], near[c]))
                for c in range(4)
            ]
            order = (0, 1, 2, 3) if face < 2 else (0, 2, 1, 3)
            sign = -1.0 if face % 2 == 0 else 1.0
            flux = numeric_flux([left[c] for c in order], [right[c] for c in order], sign)
            extra = numeric_flux([high_of[c] for c in order], [above[c] for c in order], sign)
            order = order[:3]
            for comp in range(3):
                one, two = flux[order[comp]], extra[order[comp]]
                joined = apply([table(2, n) for n in range(8)], one) + apply(
                    [table(3, n) for n in range(8)], two
                )
                change = factor * jnp.where(coarse, joined, one)
                rows = face_rows(into + comp * 64, face)
                result[rows, :] = result[rows, :] - change
        for copy in copies(block):
            copy.start()
        return carry

    lax.fori_loop(0, BLOCKS, body, 0)

    def finish(block, carry):
        for copy in copies(block):
            copy.wait()
        return carry

    lax.fori_loop(0, BLOCKS, finish, 0)


VM = pl.BlockSpec(memory_space=pltpu.VMEM)
ANY = pl.BlockSpec(memory_space=pl.ANY)


def swap(block, axis, phase):
    size = lax.axis_size(axis)
    route = [(i, (((i + phase) ^ 1) - phase) % size) for i in range(size)]
    return lax.ppermute(block, axis, route)


def on_device(depth, momentum, bed, levels, kinds, send, trace_src, back, mortar_src):
    depth = depth.reshape(64, ELEMS)
    momentum = momentum.reshape(128, ELEMS)
    bed = bed.reshape(64, ELEMS)
    levels = levels.reshape(1, ELEMS)
    mortar_src = mortar_src.reshape(8, ELEMS)
    send = jnp.pad(send, (0, 112)).reshape(1, 256)
    back = jnp.pad(back, (0, 32)).reshape(1, 128)
    message = jax.ShapeDtypeStruct((32, LANES), F32)
    state, traces, wide_a, wide_b, narrow_a, narrow_b = pl.pallas_call(
        pack_kernel,
        out_shape=(
            jax.ShapeDtypeStruct((BLOCKS * STATE, LANES), F32),
            jax.ShapeDtypeStruct((BLOCKS * TRACE, LANES), F32),
            message,
            message,
            message,
            message,
        ),
        in_specs=[ANY, ANY, ANY, VM, VM],
        out_specs=[VM] * 6,
        scratch_shapes=[pltpu.SemaphoreType.DMA((3, BLOCKS))],
        name="pack",
    )(depth, momentum, bed, send, back)
    got_wb = swap(wide_b, "wide", 1)
    got_na = swap(narrow_a, "narrow", 0)
    got_nb = swap(narrow_b, "narrow", 1)
    got_wa = swap(wide_a, "wide", 0)
    moved = pl.pallas_call(
        volume_kernel,
        out_shape=jax.ShapeDtypeStruct((BLOCKS * MOVED, LANES), F32),
        in_specs=[VM, VM],
        out_specs=VM,
        scratch_shapes=[pltpu.VMEM((192, LANES), F32)],
        name="volume",
        cost_estimate=pl.CostEstimate(flops=20_000_000, bytes_accessed=2_000_000, transcendentals=0),
    )(state, levels)
    new_depth, new_moment = pl.pallas_call(
        surface_kernel,
        out_shape=(
            jax.ShapeDtypeStruct((64, ELEMS), F32),
            jax.ShapeDtypeStruct((128, ELEMS), F32),
        ),
        in_specs=[VM] * 11,
        out_specs=[ANY, ANY],
        scratch_shapes=[pltpu.VMEM((BLOCKS * MOVED, LANES), F32), pltpu.SemaphoreType.DMA((2, BLOCKS))],
        name="surface",
    )(
        moved, traces, got_wa, got_wb, got_na, got_nb, kinds, trace_src, mortar_src, levels,
        jnp.asarray(column_tables()),
    )
    return new_depth.reshape(8, 8, ELEMS), new_moment.reshape(2, 8, 8, ELEMS)


def solution(mesh):
    both = ("wide", "narrow")
    placed = (
        P(None, None, both),
        P(None, None, None, both),
        P(None, None, both),
        P(both),
        P(None, both),
        P(both),
        P(None, both),
        P(both),
        P(None, None, both),
    )
    return jax.shard_map(
        on_device,
        mesh=mesh,
        in_specs=placed,
        out_specs=(P(None, None, both), P(None, None, None, both)),
        check_vma=False,
    )
```

```python
import jax
import jax.numpy as jnp
import numpy as np
from jax import lax
from jax.experimental import pallas as pl
from jax.experimental.pallas import tpu as pltpu
from jax.sharding import PartitionSpec as P

NODES = 8
ELEMS = 1280
LANES = 128
BLOCKS = ELEMS // LANES
TREE_BLOCKS = BLOCKS // 2
GROUPS = BLOCKS // 2
FACES = 4
STATE, TRACE, MOVED = 256, 128, 192
LOCAL = FACES * ELEMS
STEP = 0.005
F32 = jnp.float32
I32 = jnp.int32

SEND_AT = (0, 48, 96, 120)
SEND_CAP = (48, 48, 24, 24)
BACK_AT = (48, 96, 64, 80)
BACK_CAP = (32, 32, 16, 16)
RECV_OFF = (0, 48, 96, 120)
RECV_LANE = (48, 0, 120, 96)
RETN_OFF = (0, 32, 64, 80)
RETN_LANE = (96, 48, 80, 64)


def tables():
    degree = NODES - 1

    def legendre(points):
        before, current = np.ones(points.shape), points * 1.0
        for order in range(2, degree + 1):
            before, current = (
                current,
                ((2.0 * order - 1.0) * points * current - (order - 1.0) * before) / order,
            )
        return current, before

    points = -np.cos(np.pi * np.arange(NODES) / degree)
    for _ in range(100):
        top, below = legendre(points)
        points = points - (points * top - below) / (NODES * top)
    points[0], points[-1] = -1.0, 1.0
    values = legendre(points)[0]
    weights = 2.0 / (degree * NODES * values * values)
    deriv = np.zeros((NODES, NODES))
    for i in range(NODES):
        for k in range(NODES):
            if i != k:
                deriv[i, k] = values[i] / (values[k] * (points[i] - points[k]))

    def lagrange(targets):
        table = np.ones((NODES, NODES))
        for k in range(NODES):
            for o in range(NODES):
                if o != k:
                    table[:, k] = table[:, k] * (targets - points[o]) / (points[k] - points[o])
        return table

    low, high = lagrange((points - 1.0) / 2.0), lagrange((points + 1.0) / 2.0)
    proj_low = 0.5 * low.T * weights[None, :] / weights[:, None]
    proj_high = 0.5 * high.T * weights[None, :] / weights[:, None]
    return weights, deriv, low, high, proj_low, proj_high


WEIGHTS, DERIV, INTERP_LOW, INTERP_HIGH, PROJ_LOW, PROJ_HIGH = tables()
SKEW = WEIGHTS[:, None] * DERIV
LIFT = 1.0 / WEIGHTS[0]


FOLD_EVEN = 0.5 * (INTERP_LOW + INTERP_LOW[:, ::-1])[:, :4]
FOLD_ODD = 0.5 * (INTERP_LOW - INTERP_LOW[:, ::-1])[:, :4]
JOIN_SUM = 0.5 * (PROJ_LOW + PROJ_LOW[::-1])[:4]
JOIN_DIFF = 0.5 * (PROJ_LOW - PROJ_LOW[::-1])[:4]


def face_rows(base, face):
    if face == 0:
        return pl.ds(base, 8)
    if face == 1:
        return pl.ds(base + 56, 8)
    if face == 2:
        return pl.ds(base, 8, stride=8)
    return pl.ds(base + 7, 8, stride=8)


def component(face, place):
    return place if face < 2 or place in (0, 3) else 3 - place


def lanes_of(block):
    return pl.ds(pl.multiple_of(block * LANES, LANES), LANES)


def rows_of(base, count):
    return pl.ds(pl.multiple_of(base, 8), count)


def spread(row):
    return jnp.broadcast_to(row, (8, LANES))


def pick(source, lane):
    return jnp.take_along_axis(source, lane, axis=1, mode="promise_in_bounds")


def pack_kernel(
    depth, moment, bed, send, back, state, traces, wide_a, narrow_b, narrow_a, wide_b,
    send_list, back_list, sems, list_sems
):
    list_copies = [
        pltpu.make_async_copy(send, send_list, list_sems.at[0]),
        pltpu.make_async_copy(back, back_list, list_sems.at[1]),
    ]
    for copy in list_copies:
        copy.start()
    copies = []
    for block in range(BLOCKS):
        lanes = pl.ds(block * LANES, LANES)
        base = block * STATE
        for slot, (source, row, count) in enumerate(
            ((depth, 0, 64), (moment, 64, 128), (bed, 192, 64))
        ):
            copy = pltpu.make_async_copy(
                source.at[:, lanes], state.at[pl.ds(base + row, count)], sems.at[slot, block]
            )
            copy.start()
            copies.append(copy)
    for copy in list_copies:
        copy.wait()
    lane_id = lax.broadcasted_iota(I32, (8, LANES), 1)
    def full(row):
        row = row.reshape(1, row.shape[0])
        return spread(jnp.concatenate([row, jnp.zeros((1, LANES - row.shape[1]), I32)], axis=1))

    send_first = spread(send_list[pl.ds(0, LANES)].reshape(1, LANES))
    send_last = full(send_list[pl.ds(LANES, 16)])
    back_row = full(back_list[...])
    backs = (pltpu.roll(back_row, 48, 1), pltpu.roll(back_row, 64, 1), back_row, back_row)
    index = []
    for way in range(4):
        row = send_first
        if way == 3:
            row = jnp.where(lane_id < 64, send_last, send_first)
        inside = (lane_id >= BACK_AT[way]) & (lane_id < BACK_AT[way] + BACK_CAP[way])
        row = jnp.where(inside, backs[way], row)
        index.append(row - way * ELEMS)
    out = [[jnp.zeros((8, LANES), F32) for _ in range(4)] for _ in range(4)]
    lane = [row & (LANES - 1) for row in index]
    place = [row >> 7 for row in index]
    for block in range(BLOCKS):
        for copy in copies[3 * block : 3 * block + 3]:
            copy.wait()
        for way in range(4):
            here = place[way] == block
            for comp in range(4):
                piece = state[face_rows(block * STATE + component(way, comp) * 64, way), :]
                traces[pl.ds(block * TRACE + (way * 4 + comp) * 8, 8), :] = piece
                out[way][comp] = jnp.where(here, pick(piece, lane[way]), out[way][comp])
    wide_even = (lax.axis_index("wide") & 1) == 0
    narrow_even = (lax.axis_index("narrow") & 1) == 0
    for comp in range(4):
        rows = pl.ds(comp * 8, 8)
        wide_a[rows, :] = jnp.where(wide_even, out[1][comp], out[0][comp])
        wide_b[rows, :] = jnp.where(wide_even, out[0][comp], out[1][comp])
        narrow_a[rows, :] = jnp.where(narrow_even, out[3][comp], out[2][comp])
        narrow_b[rows, :] = jnp.where(narrow_even, out[2][comp], out[3][comp])


def line_terms(height, normal, tangent, bed):
    def accumulate(slot, i, value, minus=False):
        if slot[i] is None:
            slot[i] = -value if minus else value
        else:
            slot[i] = slot[i] - value if minus else slot[i] + value

    slope = [None] * 8
    for i in range(8):
        for k in range(i + 1, 8):
            bump = float(SKEW[i, k]) * (bed[k] - bed[i])
            accumulate(slope, i, bump)
            accumulate(slope, k, bump)
    square = [2.0 * (h * h) for h in height]
    mass = [None] * 8
    along = [(4.0 * height[i]) * slope[i] for i in range(8)]
    cross = [None] * 8
    for i in range(8):
        for k in range(i + 1, 8):
            q = float(SKEW[i, k])
            un = normal[i] + normal[k]
            first = (q * (height[i] + height[k])) * un
            second = first * un + q * (square[i] + square[k])
            third = first * (tangent[i] + tangent[k])
            for slot, value in ((mass, first), (along, second), (cross, third)):
                accumulate(slot, i, value)
                accumulate(slot, k, value, True)
    out = []
    for i in range(8):
        scale = STEP / WEIGHTS[i]
        out.append(
            (float(0.5 * scale) * mass[i], float(0.25 * scale) * along[i], float(0.25 * scale) * cross[i])
        )
    return out


def volume_of(state, moved, speeds, base, into, metric):
    def rows(comp, j, across):
        if across:
            return pl.ds(comp * 64 + j, 8, stride=8)
        return pl.ds(comp * 64 + j * 8, 8)

    def at(start, window):
        return pl.ds(start + window.start, window.size, window.stride)

    height = [state[at(base, rows(0, j, False)), :] for j in range(8)]
    bed = [state[at(base, rows(3, j, False)), :] for j in range(8)]
    vel_x, vel_y = [], []
    for j in range(8):
        inverse = 1.0 / height[j]
        vel_x.append(state[at(base, rows(1, j, False)), :] * inverse)
        vel_y.append(state[at(base, rows(2, j, False)), :] * inverse)
        speeds[rows(0, j, False), :] = vel_x[j]
        speeds[rows(1, j, False), :] = vel_y[j]
    terms = line_terms(height, vel_x, vel_y, bed)
    for i in range(8):
        for comp, value in enumerate(terms[i]):
            moved[at(into, rows(comp, i, False)), :] = (
                state[at(base, rows(comp, i, False)), :] - metric * value
            )
    height = [state[at(base, rows(0, j, True)), :] for j in range(8)]
    bed = [state[at(base, rows(3, j, True)), :] for j in range(8)]
    vel_x = [speeds[rows(0, j, True), :] for j in range(8)]
    vel_y = [speeds[rows(1, j, True), :] for j in range(8)]
    terms = line_terms(height, vel_y, vel_x, bed)
    for j in range(8):
        mass, along, cross = terms[j]
        for comp, value in enumerate((mass, cross, along)):
            window = at(into, rows(comp, j, True))
            moved[window, :] = moved[window, :] - metric * value


def interior_kernel(
    state, traces, kinds, trace_src, mortar_src, levels, moved, found, codes, rows_kind, rows_factor,
    speeds, picks
):
    face_id = lax.broadcasted_iota(I32, (4, LANES), 0)

    def by_face(values):
        total = jnp.full((4, LANES), values[3], I32)
        for face in range(3):
            total = jnp.where(face_id == face, values[face], total)
        return total

    home = by_face([-(face ^ 1) * ELEMS for face in range(FACES)])
    recv_shift = by_face([RECV_LANE[f] - RECV_OFF[f] - LOCAL for f in range(FACES)])
    retn_shift = by_face([RETN_LANE[f] - RETN_OFF[f] - LOCAL for f in range(FACES)])

    for tree in range(2):

        def body(step, carry, tree=tree):
            block = step + tree * TREE_BLOCKS
            lanes = lanes_of(block)
            base = pl.multiple_of(block * STATE, STATE)
            into = pl.multiple_of(block * MOVED, MOVED)
            level_row = (levels[lanes].reshape(1, LANES) + 1).astype(F32)
            kind = kinds[:, lanes]
            coarse = kind == 3
            first = jnp.where(coarse, mortar_src[0, :, lanes], trace_src[:, lanes])
            second = mortar_src[1, :, lanes]
            four = pl.ds(pl.multiple_of(block * 4, 4), 4)
            for turn, (index, shift) in enumerate(
                ((first, jnp.where(coarse, retn_shift, recv_shift)), (second, retn_shift))
            ):
                far = index >= LOCAL
                index = index + jnp.where(far, shift, home)
                lane = index & (LANES - 1)
                picks[pl.ds(turn * 8, 4), :] = lane
                picks[pl.ds(turn * 8 + 4, 4), :] = jnp.where(far, BLOCKS, index >> 7)
                codes[turn, four, :] = jnp.where(far, lane + LANES, lane)
            rows_kind[four, :] = kind
            rows_factor[four, :] = jnp.broadcast_to(level_row * float(LIFT * STEP), (4, LANES))
            for face in range(FACES):
                own = range(tree * TREE_BLOCKS, (tree + 1) * TREE_BLOCKS)
                reach = range(BLOCKS) if face == 3 - tree else own
                for turn in range(2):
                    lane = spread(picks[pl.ds(turn * 8 + face, 1), :])
                    place = spread(picks[pl.ds(turn * 8 + 4 + face, 1), :])
                    total = [None] * 4
                    for other in reach:
                        here = place == other
                        for comp in range(4):
                            row = other * TRACE + ((face ^ 1) * 4 + comp) * 8
                            got = pick(traces[pl.ds(row, 8), :], lane)
                            total[comp] = (
                                got if total[comp] is None else jnp.where(here, got, total[comp])
                            )
                    for comp in range(4):
                        row = ((turn * BLOCKS + block) * 4 + face) * 32 + comp * 8
                        found[rows_of(row, 8), :] = total[comp]
            volume_of(state, moved, speeds, base, into, spread(level_row))
            return carry

        lax.fori_loop(0, TREE_BLOCKS, body, 0)


def numeric_flux(left, right, quarter):
    inv_l, inv_r = 1.0 / left[0], 1.0 / right[0]
    un_l, un_r = left[1] * inv_l, right[1] * inv_r
    un = un_l + un_r
    ut = left[2] * inv_l + right[2] * inv_r
    half = 0.5 * jnp.maximum(
        jnp.abs(un_l) + left[0] * lax.rsqrt(left[0]), jnp.abs(un_r) + right[0] * lax.rsqrt(right[0])
    )
    first = (quarter * (left[0] + right[0])) * un
    middle = 0.5 * first
    second = middle * un + quarter * (left[0] * left[0] + right[0] * right[0])
    third = middle * ut
    return (
        first - half * ((right[0] + right[3]) - (left[0] + left[3])),
        second - half * (right[1] - left[1]),
        third - half * (right[2] - left[2]),
    )


def weighted(coefficients, values):
    total = None
    for coefficient, value in zip(coefficients, values):
        term = float(coefficient) * value
        total = term if total is None else total + term
    return total


def surface_kernel(
    moved_in, traces, found, codes, rows_kind, rows_factor, got_wa, got_nb, got_na, got_wb,
    new_depth, new_moment, moved, came, near, changes, sems
):
    del moved_in
    wide_even = (lax.axis_index("wide") & 1) == 0
    narrow_even = (lax.axis_index("narrow") & 1) == 0
    for comp in range(4):
        rows = pl.ds(comp * 8, 8)
        wide = got_wa[rows, :], got_wb[rows, :]
        narrow = got_na[rows, :], got_nb[rows, :]
        came[pl.ds(comp * 8, 8), :] = jnp.where(wide_even, wide[1], wide[0])
        came[pl.ds(32 + comp * 8, 8), :] = jnp.where(wide_even, wide[0], wide[1])
        came[pl.ds(64 + comp * 8, 8), :] = jnp.where(narrow_even, narrow[1], narrow[0])
        came[pl.ds(96 + comp * 8, 8), :] = jnp.where(narrow_even, narrow[0], narrow[1])
    row_id = lax.broadcasted_iota(I32, (8, LANES), 0)
    quarter = jnp.where((row_id & 1) == 1, 0.25, -0.25).astype(F32)

    def copies(block):
        lanes = lanes_of(block)
        row = pl.multiple_of(block * MOVED, MOVED)
        return (
            pltpu.make_async_copy(moved.at[pl.ds(row, 64)], new_depth.at[:, lanes], sems.at[0, block]),
            pltpu.make_async_copy(
                moved.at[pl.ds(row + 64, 128)], new_moment.at[:, lanes], sems.at[1, block]
            ),
        )

    def body(group, carry):
        for face in range(FACES):
            for turn in range(2):
                for half in range(2):
                    spot = half * 4 + face
                    code = spread(codes[turn, pl.ds(group * 8 + spot, 1), :])
                    far = code >= LANES
                    lane = code & (LANES - 1)
                    for comp in range(4):
                        row = ((turn * BLOCKS + group * 2 + half) * 4 + face) * 32 + comp * 8
                        there = pick(came[pl.ds(face * 32 + comp * 8, 8), :], lane)
                        near[pl.ds((turn * 4 + comp) * 64 + spot * 8, 8), :] = jnp.where(
                            far, there, found[rows_of(row, 8), :]
                        )
        eight = pl.ds(pl.multiple_of(group * 8, 8), 8)
        kind = rows_kind[eight, :]
        factor = rows_factor[eight, :]
        coarse, lower, upper = kind == 3, kind == 1, kind == 2
        left, right, high = [], [], []
        for comp in range(4):
            own = [
                traces[pl.ds(group * 256 + comp * 8 + node, 8, stride=32), :] for node in range(8)
            ]
            other = [near[pl.ds(comp * 64 + node, 8, stride=8), :] for node in range(8)]
            blend = [jnp.where(coarse, own[n], other[n]) for n in range(8)]
            even = [blend[b] + blend[7 - b] for b in range(4)]
            odd = [blend[b] - blend[7 - b] for b in range(4)]
            low_of, high_of = [None] * 8, [None] * 8
            for a in range(8):
                one, two = weighted(FOLD_EVEN[a], even), weighted(FOLD_ODD[a], odd)
                low_of[a] = one + two
                high_of[7 - a] = one - two
            left.append([jnp.where(coarse, low_of[n], own[n]) for n in range(8)])
            right.append(
                [jnp.where(lower, low_of[n], jnp.where(upper, high_of[n], other[n])) for n in range(8)]
            )
            high.append(high_of)
        one, two = [], []
        for node in range(8):
            above = [near[pl.ds((4 + comp) * 64 + node, 8, stride=8), :] for comp in range(4)]
            one.append(numeric_flux([v[node] for v in left], [v[node] for v in right], quarter))
            two.append(numeric_flux([v[node] for v in high], above, quarter))
        for comp in range(3):
            total = [one[b][comp] + two[7 - b][comp] for b in range(8)]
            differ = [one[b][comp] - two[7 - b][comp] for b in range(8)]
            for a in range(4):
                same, anti = weighted(JOIN_SUM[a], total), weighted(JOIN_DIFF[a], differ)
                for node, joined in ((a, same + anti), (7 - a, same - anti)):
                    changes[pl.ds(comp * 64 + node, 8, stride=8), :] = factor * jnp.where(
                        coarse, joined, one[node][comp]
                    )
        for half in range(2):
            into = pl.multiple_of((group * 2 + half) * MOVED, MOVED)
            for face in range(FACES):
                for comp in range(3):
                    rows = face_rows(into + component(face, comp) * 64, face)
                    moved[rows, :] = (
                        moved[rows, :] - changes[pl.ds(comp * 64 + (half * 4 + face) * 8, 8), :]
                    )
            for copy in copies(group * 2 + half):
                copy.start()
        return carry

    lax.fori_loop(0, GROUPS, body, 0)

    def finish(block, carry):
        for copy in copies(block):
            copy.wait()
        return carry

    lax.fori_loop(0, BLOCKS, finish, 0)


VM = pl.BlockSpec(memory_space=pltpu.VMEM)
FAR = pl.BlockSpec(memory_space=pltpu.HBM)
ANY = pl.BlockSpec(memory_space=pl.ANY)
PARAMS = pltpu.CompilerParams(vmem_limit_bytes=24 * 1024 * 1024)


def swap(block, axis, phase):
    size = lax.axis_size(axis)
    route = [(i, (((i + phase) ^ 1) - phase) % size) for i in range(size)]
    return lax.ppermute(block, axis, route)


def placed(memory, *arrays):
    return [pltpu.with_memory_space_constraint(array, memory) for array in arrays]


def on_device(depth, momentum, bed, levels, kinds, send, trace_src, back, mortar_src):
    depth = depth.reshape(64, ELEMS)
    momentum = momentum.reshape(128, ELEMS)
    bed = bed.reshape(64, ELEMS)
    message = pltpu.VMEM((32, LANES), F32)
    state, traces, wide_a, narrow_b, narrow_a, wide_b = pl.pallas_call(
        pack_kernel,
        out_shape=(
            pltpu.VMEM((BLOCKS * STATE, LANES), F32),
            pltpu.VMEM((BLOCKS * TRACE, LANES), F32),
            message,
            message,
            message,
            message,
        ),
        in_specs=[FAR] * 5,
        out_specs=[VM] * 6,
        scratch_shapes=[
            pltpu.VMEM((144,), I32),
            pltpu.VMEM((96,), I32),
            pltpu.SemaphoreType.DMA((3, BLOCKS)),
            pltpu.SemaphoreType.DMA((2,)),
        ],
        compiler_params=PARAMS,
        name="pack",
    )(*placed(pltpu.HBM, depth, momentum, bed, send, back))
    got_wb = swap(wide_b, "wide", 1)
    got_na = swap(narrow_a, "narrow", 0)
    got_nb = swap(narrow_b, "narrow", 1)
    got_wa = swap(wide_a, "wide", 0)
    moved, found, codes, rows_kind, rows_factor = pl.pallas_call(
        interior_kernel,
        out_shape=(
            pltpu.VMEM((BLOCKS * MOVED, LANES), F32),
            pltpu.VMEM((2 * BLOCKS * 128, LANES), F32),
            pltpu.VMEM((2, 4 * BLOCKS, LANES), I32),
            pltpu.VMEM((4 * BLOCKS, LANES), I32),
            pltpu.VMEM((4 * BLOCKS, LANES), F32),
        ),
        in_specs=[VM] * 6,
        out_specs=[VM] * 5,
        scratch_shapes=[pltpu.VMEM((128, LANES), F32), pltpu.VMEM((16, LANES), I32)],
        compiler_params=PARAMS,
        name="interior",
        cost_estimate=pl.CostEstimate(flops=20_000_000, bytes_accessed=2_000_000, transcendentals=0),
    )(*placed(pltpu.VMEM, state, traces, kinds, trace_src, mortar_src, levels))
    new_depth, new_moment, _ = pl.pallas_call(
        surface_kernel,
        out_shape=(
            jax.ShapeDtypeStruct((64, ELEMS), F32),
            jax.ShapeDtypeStruct((128, ELEMS), F32),
            pltpu.VMEM((BLOCKS * MOVED, LANES), F32),
        ),
        in_specs=[VM] * 10,
        out_specs=[ANY, ANY, VM],
        input_output_aliases={0: 2},
        scratch_shapes=[
            pltpu.VMEM((128, LANES), F32),
            pltpu.VMEM((512, LANES), F32),
            pltpu.VMEM((192, LANES), F32),
            pltpu.SemaphoreType.DMA((2, BLOCKS)),
        ],
        compiler_params=PARAMS,
        name="surface",
    )(
        *placed(
            pltpu.VMEM, moved, traces, found, codes, rows_kind, rows_factor, got_wa, got_nb, got_na, got_wb
        )
    )
    return new_depth.reshape(8, 8, ELEMS), new_moment.reshape(2, 8, 8, ELEMS)


def solution(mesh):
    both = ("wide", "narrow")
    placed = (
        P(None, None, both),
        P(None, None, None, both),
        P(None, None, both),
        P(both),
        P(None, both),
        P(both),
        P(None, both),
        P(both),
        P(None, None, both),
    )
    return jax.shard_map(
        on_device,
        mesh=mesh,
        in_specs=placed,
        out_specs=(P(None, None, both), P(None, None, None, both)),
        check_vma=False,
    )
```

```python
import jax
import jax.numpy as jnp
import numpy as np
from jax import lax
from jax.experimental import pallas as pl
from jax.experimental.pallas import tpu as pltpu
from jax.sharding import PartitionSpec as P

NODES = 8
ELEMS = 1280
LANES = 128
AHEAD = 35
BLOCKS = ELEMS // LANES
TREE_BLOCKS = BLOCKS // 2
GROUPS = BLOCKS // 2
FACES = 4
STATE, TRACE, MOVED = 256, 128, 192
LOCAL = FACES * ELEMS
STEP = 0.005
F32 = jnp.float32
I32 = jnp.int32

SEND_AT = (0, 48, 96, 120)
SEND_CAP = (48, 48, 24, 24)
BACK_AT = (48, 96, 64, 80)
BACK_CAP = (32, 32, 16, 16)
RECV_OFF = (0, 48, 96, 120)
RECV_LANE = (48, 0, 120, 96)
RETN_OFF = (0, 32, 64, 80)
RETN_LANE = (96, 48, 80, 64)


def tables():
    degree = NODES - 1

    def legendre(points):
        before, current = np.ones(points.shape), points * 1.0
        for order in range(2, degree + 1):
            before, current = (
                current,
                ((2.0 * order - 1.0) * points * current - (order - 1.0) * before) / order,
            )
        return current, before

    points = -np.cos(np.pi * np.arange(NODES) / degree)
    for _ in range(100):
        top, below = legendre(points)
        points = points - (points * top - below) / (NODES * top)
    points[0], points[-1] = -1.0, 1.0
    values = legendre(points)[0]
    weights = 2.0 / (degree * NODES * values * values)
    deriv = np.zeros((NODES, NODES))
    for i in range(NODES):
        for k in range(NODES):
            if i != k:
                deriv[i, k] = values[i] / (values[k] * (points[i] - points[k]))

    def lagrange(targets):
        table = np.ones((NODES, NODES))
        for k in range(NODES):
            for o in range(NODES):
                if o != k:
                    table[:, k] = table[:, k] * (targets - points[o]) / (points[k] - points[o])
        return table

    low, high = lagrange((points - 1.0) / 2.0), lagrange((points + 1.0) / 2.0)
    proj_low = 0.5 * low.T * weights[None, :] / weights[:, None]
    proj_high = 0.5 * high.T * weights[None, :] / weights[:, None]
    return weights, deriv, low, high, proj_low, proj_high


WEIGHTS, DERIV, INTERP_LOW, INTERP_HIGH, PROJ_LOW, PROJ_HIGH = tables()
SKEW = WEIGHTS[:, None] * DERIV
LIFT = 1.0 / WEIGHTS[0]


FOLD_EVEN = 0.5 * (INTERP_LOW + INTERP_LOW[:, ::-1])[:, :4]
FOLD_ODD = 0.5 * (INTERP_LOW - INTERP_LOW[:, ::-1])[:, :4]
JOIN_SUM = 0.5 * (PROJ_LOW + PROJ_LOW[::-1])[:4]
JOIN_DIFF = 0.5 * (PROJ_LOW - PROJ_LOW[::-1])[:4]


def face_rows(base, face):
    if face == 0:
        return pl.ds(base, 8)
    if face == 1:
        return pl.ds(base + 56, 8)
    if face == 2:
        return pl.ds(base, 8, stride=8)
    return pl.ds(base + 7, 8, stride=8)


def component(face, place):
    return place if face < 2 or place in (0, 3) else 3 - place


def lanes_of(block):
    return pl.ds(pl.multiple_of(block * LANES, LANES), LANES)


def rows_of(base, count):
    return pl.ds(pl.multiple_of(base, 8), count)


def spread(row):
    return jnp.broadcast_to(row, (8, LANES))


def pick(source, lane):
    return jnp.take_along_axis(source, lane, axis=1, mode="promise_in_bounds")


def pack_kernel(
    depth, moment, bed, send, back, kinds_far, trace_far, mortar_far, levels_far,
    state, traces, wide_a, narrow_b, narrow_a, wide_b, kinds, trace_src, mortar_src, levels,
    *rest
):
    out_refs, scratch = rest[:5], rest[5:7]
    send_list, back_list, sems, list_sems = rest[7:]
    list_copies = [
        pltpu.make_async_copy(send, send_list, list_sems.at[0]),
        pltpu.make_async_copy(back, back_list, list_sems.at[1]),
    ]
    for copy in list_copies:
        copy.start()
    copies = []
    table_copies = [
        pltpu.make_async_copy(kinds_far, kinds, list_sems.at[2]),
        pltpu.make_async_copy(trace_far, trace_src, list_sems.at[3]),
        pltpu.make_async_copy(mortar_far, mortar_src, list_sems.at[4]),
        pltpu.make_async_copy(levels_far, levels, list_sems.at[5]),
    ]
    for block in range(BLOCKS):
        lanes = pl.ds(block * LANES, LANES)
        base = block * STATE
        for slot, (source, row, count) in enumerate(
            ((depth, 0, 64), (moment, 64, 128), (bed, 192, 64))
        ):
            copy = pltpu.make_async_copy(
                source.at[:, lanes], state.at[pl.ds(base + row, count)], sems.at[slot, block]
            )
            copy.start()
            copies.append(copy)
    for copy in table_copies:
        copy.start()
    for copy in list_copies:
        copy.wait()
    lane_id = lax.broadcasted_iota(I32, (8, LANES), 1)
    def full(row):
        row = row.reshape(1, row.shape[0])
        return spread(jnp.concatenate([row, jnp.zeros((1, LANES - row.shape[1]), I32)], axis=1))

    send_first = spread(send_list[pl.ds(0, LANES)].reshape(1, LANES))
    send_last = full(send_list[pl.ds(LANES, 16)])
    back_row = full(back_list[...])
    backs = (pltpu.roll(back_row, 48, 1), pltpu.roll(back_row, 64, 1), back_row, back_row)
    index = []
    for way in range(4):
        row = send_first
        if way == 3:
            row = jnp.where(lane_id < 64, send_last, send_first)
        inside = (lane_id >= BACK_AT[way]) & (lane_id < BACK_AT[way] + BACK_CAP[way])
        row = jnp.where(inside, backs[way], row)
        index.append(row - way * ELEMS)
    out = [[jnp.zeros((8, LANES), F32) for _ in range(4)] for _ in range(4)]
    lane = [row & (LANES - 1) for row in index]
    place = [row >> 7 for row in index]
    for block in range(BLOCKS):
        for copy in copies[3 * block : 3 * block + 3]:
            copy.wait()
        for face in range(FACES):
            for comp in range(4):
                traces[pl.ds(block * TRACE + (face * 4 + comp) * 8, 8), :] = state[
                    face_rows(block * STATE + component(face, comp) * 64, face), :
                ]
    for way in range(4):
        for block in range(BLOCKS):
            here = place[way] == block
            for comp in range(4):
                got = pick(traces[pl.ds(block * TRACE + (way * 4 + comp) * 8, 8), :], lane[way])
                out[way][comp] = got if block == 0 else jnp.where(here, got, out[way][comp])
    wide_even = (lax.axis_index("wide") & 1) == 0
    narrow_even = (lax.axis_index("narrow") & 1) == 0
    for comp in range(4):
        rows = pl.ds(comp * 8, 8)
        wide_a[rows, :] = jnp.where(wide_even, out[1][comp], out[0][comp])
        wide_b[rows, :] = jnp.where(wide_even, out[0][comp], out[1][comp])
        narrow_a[rows, :] = jnp.where(narrow_even, out[3][comp], out[2][comp])
        narrow_b[rows, :] = jnp.where(narrow_even, out[2][comp], out[3][comp])
    for copy in table_copies:
        copy.wait()
    work = block_worker(state, traces, kinds, trace_src, mortar_src, levels, out_refs, scratch)

    def first_tree(block, carry):
        work(block, 0)
        return carry

    lax.fori_loop(0, blocks_ahead(), first_tree, 0)


def line_terms(height, normal, tangent, bed):
    def accumulate(slot, i, value, minus=False):
        if slot[i] is None:
            slot[i] = -value if minus else value
        else:
            slot[i] = slot[i] - value if minus else slot[i] + value

    slope = [None] * 8
    for i in range(8):
        for k in range(i + 1, 8):
            bump = float(SKEW[i, k]) * (bed[k] - bed[i])
            accumulate(slope, i, bump)
            accumulate(slope, k, bump)
        yield
    square = [2.0 * (h * h) for h in height]
    mass = [None] * 8
    along = [(4.0 * height[i]) * slope[i] for i in range(8)]
    cross = [None] * 8
    for i in range(8):
        for k in range(i + 1, 8):
            q = float(SKEW[i, k])
            un = normal[i] + normal[k]
            first = (q * (height[i] + height[k])) * un
            second = first * un + q * (square[i] + square[k])
            third = first * (tangent[i] + tangent[k])
            for slot, value in ((mass, first), (along, second), (cross, third)):
                accumulate(slot, i, value)
                accumulate(slot, k, value, True)
            yield
    out = []
    for i in range(8):
        scale = STEP / WEIGHTS[i]
        out.append(
            (float(0.5 * scale) * mass[i], float(0.25 * scale) * along[i], float(0.25 * scale) * cross[i])
        )
    return out


def volume_of(state, moved, speeds, base, into, metric):
    def rows(comp, j, across):
        if across:
            return pl.ds(comp * 64 + j, 8, stride=8)
        return pl.ds(comp * 64 + j * 8, 8)

    def at(start, window):
        return pl.ds(start + window.start, window.size, window.stride)

    height = [state[at(base, rows(0, j, False)), :] for j in range(8)]
    bed = [state[at(base, rows(3, j, False)), :] for j in range(8)]
    vel_x, vel_y = [], []
    for j in range(8):
        inverse = 1.0 / height[j]
        vel_x.append(state[at(base, rows(1, j, False)), :] * inverse)
        vel_y.append(state[at(base, rows(2, j, False)), :] * inverse)
        speeds[rows(0, j, False), :] = vel_x[j]
        speeds[rows(1, j, False), :] = vel_y[j]
    terms = yield from line_terms(height, vel_x, vel_y, bed)
    for i in range(8):
        for comp, value in enumerate(terms[i]):
            moved[at(into, rows(comp, i, False)), :] = (
                state[at(base, rows(comp, i, False)), :] - metric * value
            )
    height = [state[at(base, rows(0, j, True)), :] for j in range(8)]
    bed = [state[at(base, rows(3, j, True)), :] for j in range(8)]
    vel_x = [speeds[rows(0, j, True), :] for j in range(8)]
    vel_y = [speeds[rows(1, j, True), :] for j in range(8)]
    terms = yield from line_terms(height, vel_y, vel_x, bed)
    for j in range(8):
        mass, along, cross = terms[j]
        for comp, value in enumerate((mass, cross, along)):
            window = at(into, rows(comp, j, True))
            moved[window, :] = moved[window, :] - metric * value


def gather_of(traces, found, picks, block, tree):
    for face in range(FACES):
        own = range(tree * TREE_BLOCKS, (tree + 1) * TREE_BLOCKS)
        reach = range(BLOCKS) if face == 3 - tree else own
        for turn in range(2):
            lane = spread(picks[pl.ds(turn * 8 + face, 1), :])
            place = spread(picks[pl.ds(turn * 8 + 4 + face, 1), :])
            total = [None] * 4
            for other in reach:
                here = place == other
                for comp in range(4):
                    row = other * TRACE + ((face ^ 1) * 4 + comp) * 8
                    got = pick(traces[pl.ds(row, 8), :], lane)
                    total[comp] = got if total[comp] is None else jnp.where(here, got, total[comp])
                yield
            for comp in range(4):
                row = ((turn * BLOCKS + block) * 4 + face) * 32 + comp * 8
                found[rows_of(row, 8), :] = total[comp]


def interleave(*works):
    works = list(works)
    while works:
        for work in list(works):
            if next(work, works) is works:
                works.remove(work)


def block_worker(state, traces, kinds, trace_src, mortar_src, levels, out, scratch):
    moved, found, codes, rows_kind, rows_factor = out
    speeds, picks = scratch
    face_id = lax.broadcasted_iota(I32, (4, LANES), 0)

    def by_face(values):
        total = jnp.full((4, LANES), values[3], I32)
        for face in range(3):
            total = jnp.where(face_id == face, values[face], total)
        return total

    home = by_face([-(face ^ 1) * ELEMS for face in range(FACES)])
    recv_shift = by_face([RECV_LANE[f] - RECV_OFF[f] - LOCAL for f in range(FACES)])
    retn_shift = by_face([RETN_LANE[f] - RETN_OFF[f] - LOCAL for f in range(FACES)])

    def work(block, tree):
        lanes = lanes_of(block)
        base = pl.multiple_of(block * STATE, STATE)
        into = pl.multiple_of(block * MOVED, MOVED)
        level_row = (levels[lanes].reshape(1, LANES) + 1).astype(F32)
        kind = kinds[:, lanes]
        coarse = kind == 3
        first = jnp.where(coarse, mortar_src[0, :, lanes], trace_src[:, lanes])
        second = mortar_src[1, :, lanes]
        four = pl.ds(pl.multiple_of(block * 4, 4), 4)
        for turn, (index, shift) in enumerate(
            ((first, jnp.where(coarse, retn_shift, recv_shift)), (second, retn_shift))
        ):
            far = index >= LOCAL
            index = index + jnp.where(far, shift, home)
            lane = index & (LANES - 1)
            picks[pl.ds(turn * 8, 4), :] = lane
            picks[pl.ds(turn * 8 + 4, 4), :] = jnp.where(far, BLOCKS, index >> 7)
            codes[turn, four, :] = jnp.where(far, lane + LANES, lane)
        rows_kind[four, :] = kind
        rows_factor[four, :] = jnp.broadcast_to(level_row * float(LIFT * STEP), (4, LANES))
        interleave(
            volume_of(state, moved, speeds, base, into, spread(level_row)),
            gather_of(traces, found, picks, block, tree),
        )

    return work


def blocks_ahead():
    wide, narrow = lax.axis_index("wide"), lax.axis_index("narrow")
    x, z, core = wide >> 3, (wide >> 1) & 3, wide & 1

    def one_of(at, values):
        total = jnp.int32(values[3])
        for i in range(3):
            total = jnp.where(at == i, jnp.int32(values[i]), total)
        return total

    lead = AHEAD - one_of(narrow, (0, 7, 15, 19)) - one_of(x, (0, 10, 12, 14)) - one_of(z, (0, 10, 22, 26))
    return jnp.clip((lead + 5 * core) // 5, 0, TREE_BLOCKS)


def interior_kernel(
    state, traces, kinds, trace_src, mortar_src, levels, *rest
):
    out, scratch = rest[5:10], rest[10:]
    work = block_worker(state, traces, kinds, trace_src, mortar_src, levels, out, scratch)

    def first_tree(block, carry):
        work(block, 0)
        return carry

    def second_tree(block, carry):
        work(block, 1)
        return carry

    lax.fori_loop(blocks_ahead(), TREE_BLOCKS, first_tree, 0)
    lax.fori_loop(TREE_BLOCKS, BLOCKS, second_tree, 0)


def numeric_flux(left, right, quarter):
    inv_l, inv_r = 1.0 / left[0], 1.0 / right[0]
    un_l, un_r = left[1] * inv_l, right[1] * inv_r
    un = un_l + un_r
    ut = left[2] * inv_l + right[2] * inv_r
    half = 0.5 * jnp.maximum(
        jnp.abs(un_l) + left[0] * lax.rsqrt(left[0]), jnp.abs(un_r) + right[0] * lax.rsqrt(right[0])
    )
    first = (quarter * (left[0] + right[0])) * un
    middle = 0.5 * first
    second = middle * un + quarter * (left[0] * left[0] + right[0] * right[0])
    third = middle * ut
    return (
        first - half * ((right[0] + right[3]) - (left[0] + left[3])),
        second - half * (right[1] - left[1]),
        third - half * (right[2] - left[2]),
    )


def weighted(coefficients, values):
    total = None
    for coefficient, value in zip(coefficients, values):
        term = float(coefficient) * value
        total = term if total is None else total + term
    return total


def surface_kernel(
    moved_in, traces, found, codes, rows_kind, rows_factor, got_wa, got_nb, got_na, got_wb,
    new_depth, new_moment, moved, came, near, changes, sems
):
    del moved_in
    wide_even = (lax.axis_index("wide") & 1) == 0
    narrow_even = (lax.axis_index("narrow") & 1) == 0
    for comp in range(4):
        rows = pl.ds(comp * 8, 8)
        wide = got_wa[rows, :], got_wb[rows, :]
        narrow = got_na[rows, :], got_nb[rows, :]
        came[pl.ds(comp * 8, 8), :] = jnp.where(wide_even, wide[1], wide[0])
        came[pl.ds(32 + comp * 8, 8), :] = jnp.where(wide_even, wide[0], wide[1])
        came[pl.ds(64 + comp * 8, 8), :] = jnp.where(narrow_even, narrow[1], narrow[0])
        came[pl.ds(96 + comp * 8, 8), :] = jnp.where(narrow_even, narrow[0], narrow[1])
    row_id = lax.broadcasted_iota(I32, (8, LANES), 0)
    quarter = jnp.where((row_id & 1) == 1, 0.25, -0.25).astype(F32)

    def copies(block):
        lanes = lanes_of(block)
        row = pl.multiple_of(block * MOVED, MOVED)
        return (
            pltpu.make_async_copy(moved.at[pl.ds(row, 64)], new_depth.at[:, lanes], sems.at[0, block]),
            pltpu.make_async_copy(
                moved.at[pl.ds(row + 64, 128)], new_moment.at[:, lanes], sems.at[1, block]
            ),
        )

    def body(group, carry):
        for face in range(FACES):
            for turn in range(2):
                for half in range(2):
                    spot = half * 4 + face
                    code = spread(codes[turn, pl.ds(group * 8 + spot, 1), :])
                    far = code >= LANES
                    lane = code & (LANES - 1)
                    for comp in range(4):
                        row = ((turn * BLOCKS + group * 2 + half) * 4 + face) * 32 + comp * 8
                        there = pick(came[pl.ds(face * 32 + comp * 8, 8), :], lane)
                        near[pl.ds((turn * 4 + comp) * 64 + spot * 8, 8), :] = jnp.where(
                            far, there, found[rows_of(row, 8), :]
                        )
        eight = pl.ds(pl.multiple_of(group * 8, 8), 8)
        kind = rows_kind[eight, :]
        factor = rows_factor[eight, :]
        coarse, lower, upper = kind == 3, kind == 1, kind == 2
        left, right, high = [], [], []
        for comp in range(4):
            own = [
                traces[pl.ds(group * 256 + comp * 8 + node, 8, stride=32), :] for node in range(8)
            ]
            other = [near[pl.ds(comp * 64 + node, 8, stride=8), :] for node in range(8)]
            blend = [jnp.where(coarse, own[n], other[n]) for n in range(8)]
            even = [blend[b] + blend[7 - b] for b in range(4)]
            odd = [blend[b] - blend[7 - b] for b in range(4)]
            low_of, high_of = [None] * 8, [None] * 8
            for a in range(8):
                one, two = weighted(FOLD_EVEN[a], even), weighted(FOLD_ODD[a], odd)
                low_of[a] = one + two
                high_of[7 - a] = one - two
            left.append([jnp.where(coarse, low_of[n], own[n]) for n in range(8)])
            right.append(
                [jnp.where(lower, low_of[n], jnp.where(upper, high_of[n], other[n])) for n in range(8)]
            )
            high.append(high_of)
        one, two = [], []
        for node in range(8):
            above = [near[pl.ds((4 + comp) * 64 + node, 8, stride=8), :] for comp in range(4)]
            one.append(numeric_flux([v[node] for v in left], [v[node] for v in right], quarter))
            two.append(numeric_flux([v[node] for v in high], above, quarter))
        for comp in range(3):
            total = [one[b][comp] + two[7 - b][comp] for b in range(8)]
            differ = [one[b][comp] - two[7 - b][comp] for b in range(8)]
            for a in range(4):
                same, anti = weighted(JOIN_SUM[a], total), weighted(JOIN_DIFF[a], differ)
                for node, joined in ((a, same + anti), (7 - a, same - anti)):
                    changes[pl.ds(comp * 64 + node, 8, stride=8), :] = factor * jnp.where(
                        coarse, joined, one[node][comp]
                    )
        for half in range(2):
            into = pl.multiple_of((group * 2 + half) * MOVED, MOVED)
            for face in range(FACES):
                for comp in range(3):
                    rows = face_rows(into + component(face, comp) * 64, face)
                    moved[rows, :] = (
                        moved[rows, :] - changes[pl.ds(comp * 64 + (half * 4 + face) * 8, 8), :]
                    )
            for copy in copies(group * 2 + half):
                copy.start()
        return carry

    lax.fori_loop(0, GROUPS, body, 0)

    def finish(block, carry):
        for copy in copies(block):
            copy.wait()
        return carry

    lax.fori_loop(0, BLOCKS, finish, 0)


VM = pl.BlockSpec(memory_space=pltpu.VMEM)
FAR = pl.BlockSpec(memory_space=pltpu.HBM)
ANY = pl.BlockSpec(memory_space=pl.ANY)
PARAMS = pltpu.CompilerParams(vmem_limit_bytes=24 * 1024 * 1024)


def swap(block, axis, phase):
    size = lax.axis_size(axis)
    route = [(i, (((i + phase) ^ 1) - phase) % size) for i in range(size)]
    return lax.ppermute(block, axis, route)


def placed(memory, *arrays):
    return [pltpu.with_memory_space_constraint(array, memory) for array in arrays]


def on_device(depth, momentum, bed, levels, kinds, send, trace_src, back, mortar_src):
    depth = depth.reshape(64, ELEMS)
    momentum = momentum.reshape(128, ELEMS)
    bed = bed.reshape(64, ELEMS)
    message = pltpu.VMEM((32, LANES), F32)
    tables = (
        pltpu.VMEM((4, ELEMS), I32),
        pltpu.VMEM((4, ELEMS), I32),
        pltpu.VMEM((2, 4, ELEMS), I32),
        pltpu.VMEM((ELEMS,), I32),
    )
    done = (
        pltpu.VMEM((BLOCKS * MOVED, LANES), F32),
        pltpu.VMEM((2 * BLOCKS * 128, LANES), F32),
        pltpu.VMEM((2, 4 * BLOCKS, LANES), I32),
        pltpu.VMEM((4 * BLOCKS, LANES), I32),
        pltpu.VMEM((4 * BLOCKS, LANES), F32),
    )
    held = pltpu.VMEM((BLOCKS * STATE, LANES), F32), pltpu.VMEM((BLOCKS * TRACE, LANES), F32)
    work_space = [pltpu.VMEM((128, LANES), F32), pltpu.VMEM((16, LANES), I32)]
    packed = pl.pallas_call(
        pack_kernel,
        out_shape=held + (message,) * 4 + tables + done,
        in_specs=[FAR] * 9,
        out_specs=[VM] * 15,
        scratch_shapes=work_space
        + [
            pltpu.VMEM((144,), I32),
            pltpu.VMEM((96,), I32),
            pltpu.SemaphoreType.DMA((3, BLOCKS)),
            pltpu.SemaphoreType.DMA((6,)),
        ],
        compiler_params=PARAMS,
        name="pack",
    )(*placed(pltpu.HBM, depth, momentum, bed, send, back, kinds, trace_src, mortar_src, levels))
    state, traces = packed[:2]
    wide_a, narrow_b, narrow_a, wide_b = packed[2:6]
    got_wb = swap(wide_b, "wide", 1)
    got_na = swap(narrow_a, "narrow", 0)
    got_nb = swap(narrow_b, "narrow", 1)
    got_wa = swap(wide_a, "wide", 0)
    moved, found, codes, rows_kind, rows_factor = pl.pallas_call(
        interior_kernel,
        out_shape=done,
        in_specs=[VM] * 11,
        out_specs=[VM] * 5,
        input_output_aliases={6 + i: i for i in range(5)},
        scratch_shapes=work_space,
        compiler_params=PARAMS,
        name="interior",
        cost_estimate=pl.CostEstimate(flops=20_000_000, bytes_accessed=2_000_000, transcendentals=0),
    )(*placed(pltpu.VMEM, state, traces, *packed[6:15]))
    new_depth, new_moment, _ = pl.pallas_call(
        surface_kernel,
        out_shape=(
            jax.ShapeDtypeStruct((64, ELEMS), F32),
            jax.ShapeDtypeStruct((128, ELEMS), F32),
            pltpu.VMEM((BLOCKS * MOVED, LANES), F32),
        ),
        in_specs=[VM] * 10,
        out_specs=[ANY, ANY, VM],
        input_output_aliases={0: 2},
        scratch_shapes=[
            pltpu.VMEM((128, LANES), F32),
            pltpu.VMEM((512, LANES), F32),
            pltpu.VMEM((192, LANES), F32),
            pltpu.SemaphoreType.DMA((2, BLOCKS)),
        ],
        compiler_params=PARAMS,
        name="surface",
    )(
        *placed(
            pltpu.VMEM, moved, traces, found, codes, rows_kind, rows_factor, got_wa, got_nb, got_na, got_wb
        )
    )
    return new_depth.reshape(8, 8, ELEMS), new_moment.reshape(2, 8, 8, ELEMS)


def solution(mesh):
    both = ("wide", "narrow")
    placed = (
        P(None, None, both),
        P(None, None, None, both),
        P(None, None, both),
        P(both),
        P(None, both),
        P(both),
        P(None, both),
        P(both),
        P(None, None, both),
    )
    return jax.shard_map(
        on_device,
        mesh=mesh,
        in_specs=placed,
        out_specs=(P(None, None, both), P(None, None, None, both)),
        check_vma=False,
    )
```

```python
import jax
import jax.numpy as jnp
import numpy as np
from jax import lax
from jax.experimental import pallas as pl
from jax.experimental.pallas import tpu as pltpu
from jax.sharding import PartitionSpec as P

NODES = 8
ELEMS = 1280
LANES = 128
AHEAD = 35
PER_BLOCK = 5
BLOCKS = ELEMS // LANES
TREE_BLOCKS = BLOCKS // 2
GROUPS = BLOCKS // 2
FACES = 4
STATE, TRACE, MOVED = 256, 128, 192
LOCAL = FACES * ELEMS
STEP = 0.005
F32 = jnp.float32
I32 = jnp.int32

SEND_AT = (0, 48, 96, 120)
SEND_CAP = (48, 48, 24, 24)
BACK_AT = (48, 96, 64, 80)
BACK_CAP = (32, 32, 16, 16)
RECV_OFF = (0, 48, 96, 120)
RECV_LANE = (48, 0, 120, 96)
RETN_OFF = (0, 32, 64, 80)
RETN_LANE = (96, 48, 80, 64)


def tables():
    degree = NODES - 1

    def legendre(points):
        before, current = np.ones(points.shape), points * 1.0
        for order in range(2, degree + 1):
            before, current = (
                current,
                ((2.0 * order - 1.0) * points * current - (order - 1.0) * before) / order,
            )
        return current, before

    points = -np.cos(np.pi * np.arange(NODES) / degree)
    for _ in range(100):
        top, below = legendre(points)
        points = points - (points * top - below) / (NODES * top)
    points[0], points[-1] = -1.0, 1.0
    values = legendre(points)[0]
    weights = 2.0 / (degree * NODES * values * values)
    deriv = np.zeros((NODES, NODES))
    for i in range(NODES):
        for k in range(NODES):
            if i != k:
                deriv[i, k] = values[i] / (values[k] * (points[i] - points[k]))

    def lagrange(targets):
        table = np.ones((NODES, NODES))
        for k in range(NODES):
            for o in range(NODES):
                if o != k:
                    table[:, k] = table[:, k] * (targets - points[o]) / (points[k] - points[o])
        return table

    low, high = lagrange((points - 1.0) / 2.0), lagrange((points + 1.0) / 2.0)
    proj_low = 0.5 * low.T * weights[None, :] / weights[:, None]
    proj_high = 0.5 * high.T * weights[None, :] / weights[:, None]
    return weights, deriv, low, high, proj_low, proj_high


WEIGHTS, DERIV, INTERP_LOW, INTERP_HIGH, PROJ_LOW, PROJ_HIGH = tables()
SKEW = WEIGHTS[:, None] * DERIV
LIFT = 1.0 / WEIGHTS[0]


FOLD_EVEN = 0.5 * (INTERP_LOW + INTERP_LOW[:, ::-1])[:, :4]
FOLD_ODD = 0.5 * (INTERP_LOW - INTERP_LOW[:, ::-1])[:, :4]
JOIN_SUM = 0.5 * (PROJ_LOW + PROJ_LOW[::-1])[:4]
JOIN_DIFF = 0.5 * (PROJ_LOW - PROJ_LOW[::-1])[:4]


def face_rows(base, face):
    if face == 0:
        return pl.ds(base, 8)
    if face == 1:
        return pl.ds(base + 56, 8)
    if face == 2:
        return pl.ds(base, 8, stride=8)
    return pl.ds(base + 7, 8, stride=8)


def component(face, place):
    return place if face < 2 or place in (0, 3) else 3 - place


def lanes_of(block):
    return pl.ds(pl.multiple_of(block * LANES, LANES), LANES)


def rows_of(base, count):
    return pl.ds(pl.multiple_of(base, 8), count)


def spread(row):
    return jnp.broadcast_to(row, (8, LANES))


def pick(source, lane):
    return jnp.take_along_axis(source, lane, axis=1, mode="promise_in_bounds")


def pack_kernel(
    depth, moment, bed, send, back, kinds_far, trace_far, mortar_far, levels_far,
    state, traces, wide_a, narrow_b, narrow_a, wide_b, kinds, trace_src, mortar_src, levels,
    *rest
):
    out_refs, scratch = rest[:5], rest[5:7]
    send_list, back_list, sems, list_sems = rest[7:]
    list_copies = [
        pltpu.make_async_copy(send, send_list, list_sems.at[0]),
        pltpu.make_async_copy(back, back_list, list_sems.at[1]),
    ]
    for copy in list_copies:
        copy.start()
    copies = []
    table_copies = [
        pltpu.make_async_copy(kinds_far, kinds, list_sems.at[2]),
        pltpu.make_async_copy(trace_far, trace_src, list_sems.at[3]),
        pltpu.make_async_copy(mortar_far, mortar_src, list_sems.at[4]),
        pltpu.make_async_copy(levels_far, levels, list_sems.at[5]),
    ]
    for block in range(BLOCKS):
        lanes = pl.ds(block * LANES, LANES)
        base = block * STATE
        for slot, (source, row, count) in enumerate(
            ((depth, 0, 64), (moment, 64, 128), (bed, 192, 64))
        ):
            copy = pltpu.make_async_copy(
                source.at[:, lanes], state.at[pl.ds(base + row, count)], sems.at[slot, block]
            )
            copy.start()
            copies.append(copy)
    for copy in table_copies:
        copy.start()
    for copy in list_copies:
        copy.wait()
    lane_id = lax.broadcasted_iota(I32, (8, LANES), 1)
    def full(row):
        row = row.reshape(1, row.shape[0])
        return spread(jnp.concatenate([row, jnp.zeros((1, LANES - row.shape[1]), I32)], axis=1))

    send_first = spread(send_list[pl.ds(0, LANES)].reshape(1, LANES))
    send_last = full(send_list[pl.ds(LANES, 16)])
    back_row = full(back_list[...])
    backs = (pltpu.roll(back_row, 48, 1), pltpu.roll(back_row, 64, 1), back_row, back_row)
    index = []
    for way in range(4):
        row = send_first
        if way == 3:
            row = jnp.where(lane_id < 64, send_last, send_first)
        inside = (lane_id >= BACK_AT[way]) & (lane_id < BACK_AT[way] + BACK_CAP[way])
        row = jnp.where(inside, backs[way], row)
        index.append(row - way * ELEMS)
    out = [[jnp.zeros((8, LANES), F32) for _ in range(4)] for _ in range(4)]
    lane = [row & (LANES - 1) for row in index]
    place = [row >> 7 for row in index]
    for block in range(BLOCKS):
        for copy in copies[3 * block : 3 * block + 3]:
            copy.wait()
        for face in range(FACES):
            for comp in range(4):
                traces[pl.ds(block * TRACE + (face * 4 + comp) * 8, 8), :] = state[
                    face_rows(block * STATE + component(face, comp) * 64, face), :
                ]
    for way in range(4):
        for block in range(BLOCKS):
            here = place[way] == block
            for comp in range(4):
                got = pick(traces[pl.ds(block * TRACE + (way * 4 + comp) * 8, 8), :], lane[way])
                out[way][comp] = got if block == 0 else jnp.where(here, got, out[way][comp])
    wide_even = (lax.axis_index("wide") & 1) == 0
    narrow_even = (lax.axis_index("narrow") & 1) == 0
    for comp in range(4):
        rows = pl.ds(comp * 8, 8)
        wide_a[rows, :] = jnp.where(wide_even, out[1][comp], out[0][comp])
        wide_b[rows, :] = jnp.where(wide_even, out[0][comp], out[1][comp])
        narrow_a[rows, :] = jnp.where(narrow_even, out[3][comp], out[2][comp])
        narrow_b[rows, :] = jnp.where(narrow_even, out[2][comp], out[3][comp])
    for copy in table_copies:
        copy.wait()
    work = block_worker(state, traces, kinds, trace_src, mortar_src, levels, out_refs, scratch)

    def first_tree(block, carry):
        work(block, 0)
        return carry

    lax.fori_loop(0, blocks_ahead(), first_tree, 0)


def line_terms(height, normal, tangent, bed, marks):
    def accumulate(slot, i, value, minus=False):
        if slot[i] is None:
            slot[i] = -value if minus else value
        else:
            slot[i] = slot[i] - value if minus else slot[i] + value

    slope = [None] * 8
    for i in range(8):
        for k in range(i + 1, 8):
            bump = float(SKEW[i, k]) * (bed[k] - bed[i])
            accumulate(slope, i, bump)
            accumulate(slope, k, bump)
        yield
    square = [2.0 * (h * h) for h in height]
    mass = [None] * 8
    along = [(4.0 * height[i]) * slope[i] for i in range(8)]
    cross = [None] * 8
    for i in range(8):
        for k in range(i + 1, 8):
            q = float(SKEW[i, k])
            un = normal[i] + normal[k]
            if marks:
                un = un + marks.pop(0)
            first = (q * (height[i] + height[k])) * un
            second = first * un + q * (square[i] + square[k])
            third = first * (tangent[i] + tangent[k])
            for slot, value in ((mass, first), (along, second), (cross, third)):
                accumulate(slot, i, value)
                accumulate(slot, k, value, True)
            yield
    out = []
    for i in range(8):
        scale = STEP / WEIGHTS[i]
        out.append(
            (float(0.5 * scale) * mass[i], float(0.25 * scale) * along[i], float(0.25 * scale) * cross[i])
        )
    return out


def volume_of(state, moved, speeds, base, into, metric, marks):
    def rows(comp, j, across):
        if across:
            return pl.ds(comp * 64 + j, 8, stride=8)
        return pl.ds(comp * 64 + j * 8, 8)

    def at(start, window):
        return pl.ds(start + window.start, window.size, window.stride)

    height = [state[at(base, rows(0, j, False)), :] for j in range(8)]
    bed = [state[at(base, rows(3, j, False)), :] for j in range(8)]
    vel_x, vel_y = [], []
    for j in range(8):
        inverse = 1.0 / height[j]
        vel_x.append(state[at(base, rows(1, j, False)), :] * inverse)
        vel_y.append(state[at(base, rows(2, j, False)), :] * inverse)
        speeds[rows(0, j, False), :] = vel_x[j]
        speeds[rows(1, j, False), :] = vel_y[j]
    terms = yield from line_terms(height, vel_x, vel_y, bed, marks)
    for i in range(8):
        for comp, value in enumerate(terms[i]):
            moved[at(into, rows(comp, i, False)), :] = (
                state[at(base, rows(comp, i, False)), :] - metric * value
            )
    height = [state[at(base, rows(0, j, True)), :] for j in range(8)]
    bed = [state[at(base, rows(3, j, True)), :] for j in range(8)]
    vel_x = [speeds[rows(0, j, True), :] for j in range(8)]
    vel_y = [speeds[rows(1, j, True), :] for j in range(8)]
    terms = yield from line_terms(height, vel_y, vel_x, bed, marks)
    for j in range(8):
        mass, along, cross = terms[j]
        for comp, value in enumerate((mass, cross, along)):
            window = at(into, rows(comp, j, True))
            moved[window, :] = moved[window, :] - metric * value


def gather_of(traces, found, picks, block, tree, marks):
    for face in range(FACES):
        own = range(tree * TREE_BLOCKS, (tree + 1) * TREE_BLOCKS)
        reach = range(BLOCKS) if face == 3 - tree else own
        for turn in range(2):
            lane = spread(picks[pl.ds(turn * 8 + face, 1), :])
            place = spread(picks[pl.ds(turn * 8 + 4 + face, 1), :])
            total = [None] * 4
            for other in reach:
                here = place == other
                for comp in range(4):
                    row = other * TRACE + ((face ^ 1) * 4 + comp) * 8
                    got = pick(traces[pl.ds(row, 8), :], lane)
                    total[comp] = got if total[comp] is None else jnp.where(here, got, total[comp])
                yield
            for comp in range(4):
                row = ((turn * BLOCKS + block) * 4 + face) * 32 + comp * 8
                found[rows_of(row, 8), :] = total[comp]
            marks.append(0.0 * total[3])


def interleave(*works):
    works = list(works)
    while works:
        for work in list(works):
            if next(work, works) is works:
                works.remove(work)


def block_worker(state, traces, kinds, trace_src, mortar_src, levels, out, scratch):
    moved, found, codes, rows_kind, rows_factor = out
    speeds, picks = scratch
    face_id = lax.broadcasted_iota(I32, (4, LANES), 0)

    def by_face(values):
        total = jnp.full((4, LANES), values[3], I32)
        for face in range(3):
            total = jnp.where(face_id == face, values[face], total)
        return total

    home = by_face([-(face ^ 1) * ELEMS for face in range(FACES)])
    recv_shift = by_face([RECV_LANE[f] - RECV_OFF[f] - LOCAL for f in range(FACES)])
    retn_shift = by_face([RETN_LANE[f] - RETN_OFF[f] - LOCAL for f in range(FACES)])

    def work(block, tree):
        lanes = lanes_of(block)
        base = pl.multiple_of(block * STATE, STATE)
        into = pl.multiple_of(block * MOVED, MOVED)
        level_row = (levels[lanes].reshape(1, LANES) + 1).astype(F32)
        kind = kinds[:, lanes]
        coarse = kind == 3
        first = jnp.where(coarse, mortar_src[0, :, lanes], trace_src[:, lanes])
        second = mortar_src[1, :, lanes]
        four = pl.ds(pl.multiple_of(block * 4, 4), 4)
        for turn, (index, shift) in enumerate(
            ((first, jnp.where(coarse, retn_shift, recv_shift)), (second, retn_shift))
        ):
            far = index >= LOCAL
            index = index + jnp.where(far, shift, home)
            lane = index & (LANES - 1)
            picks[pl.ds(turn * 8, 4), :] = lane
            picks[pl.ds(turn * 8 + 4, 4), :] = jnp.where(far, BLOCKS, index >> 7)
            codes[turn, four, :] = jnp.where(far, lane + LANES, lane)
        rows_kind[four, :] = kind
        rows_factor[four, :] = jnp.broadcast_to(level_row * float(LIFT * STEP), (4, LANES))
        marks = []
        interleave(
            gather_of(traces, found, picks, block, tree, marks),
            volume_of(state, moved, speeds, base, into, spread(level_row), marks),
        )

    return work


def blocks_ahead():
    wide, narrow = lax.axis_index("wide"), lax.axis_index("narrow")
    x, z, core = wide >> 3, (wide >> 1) & 3, wide & 1

    def one_of(at, values):
        total = jnp.int32(values[3])
        for i in range(3):
            total = jnp.where(at == i, jnp.int32(values[i]), total)
        return total

    lead = AHEAD - one_of(narrow, (0, 7, 15, 19)) - one_of(x, (0, 10, 12, 14)) - one_of(z, (0, 10, 22, 26))
    return jnp.clip((lead + 5 * core) // PER_BLOCK, 0, TREE_BLOCKS)


def interior_kernel(
    state, traces, kinds, trace_src, mortar_src, levels, *rest
):
    out, scratch = rest[5:10], rest[10:]
    work = block_worker(state, traces, kinds, trace_src, mortar_src, levels, out, scratch)

    def first_tree(block, carry):
        work(block, 0)
        return carry

    def second_tree(block, carry):
        work(block, 1)
        return carry

    lax.fori_loop(blocks_ahead(), TREE_BLOCKS, first_tree, 0)
    lax.fori_loop(TREE_BLOCKS, BLOCKS, second_tree, 0)


def numeric_flux(left, right, quarter):
    inv_l, inv_r = 1.0 / left[0], 1.0 / right[0]
    un_l, un_r = left[1] * inv_l, right[1] * inv_r
    un = un_l + un_r
    ut = left[2] * inv_l + right[2] * inv_r
    half = 0.5 * jnp.maximum(
        jnp.abs(un_l) + left[0] * lax.rsqrt(left[0]), jnp.abs(un_r) + right[0] * lax.rsqrt(right[0])
    )
    first = (quarter * (left[0] + right[0])) * un
    middle = 0.5 * first
    second = middle * un + quarter * (left[0] * left[0] + right[0] * right[0])
    third = middle * ut
    return (
        first - half * ((right[0] + right[3]) - (left[0] + left[3])),
        second - half * (right[1] - left[1]),
        third - half * (right[2] - left[2]),
    )


def weighted(coefficients, values):
    total = None
    for coefficient, value in zip(coefficients, values):
        term = float(coefficient) * value
        total = term if total is None else total + term
    return total


def surface_kernel(
    moved_in, traces, found, codes, rows_kind, rows_factor, got_wa, got_nb, got_na, got_wb,
    new_depth, new_moment, moved, came, near_a, near_b, changes, sems
):
    del moved_in
    wide_even = (lax.axis_index("wide") & 1) == 0
    narrow_even = (lax.axis_index("narrow") & 1) == 0
    for comp in range(4):
        rows = pl.ds(comp * 8, 8)
        wide = got_wa[rows, :], got_wb[rows, :]
        narrow = got_na[rows, :], got_nb[rows, :]
        came[pl.ds(comp * 8, 8), :] = jnp.where(wide_even, wide[1], wide[0])
        came[pl.ds(32 + comp * 8, 8), :] = jnp.where(wide_even, wide[0], wide[1])
        came[pl.ds(64 + comp * 8, 8), :] = jnp.where(narrow_even, narrow[1], narrow[0])
        came[pl.ds(96 + comp * 8, 8), :] = jnp.where(narrow_even, narrow[0], narrow[1])
    row_id = lax.broadcasted_iota(I32, (8, LANES), 0)
    quarter = jnp.where((row_id & 1) == 1, 0.25, -0.25).astype(F32)

    def copies(block):
        lanes = lanes_of(block)
        row = pl.multiple_of(block * MOVED, MOVED)
        return (
            pltpu.make_async_copy(moved.at[pl.ds(row, 64)], new_depth.at[:, lanes], sems.at[0, block]),
            pltpu.make_async_copy(
                moved.at[pl.ds(row + 64, 128)], new_moment.at[:, lanes], sems.at[1, block]
            ),
        )

    def fetch(group, near, marks):
        for face in range(FACES):
            for turn in range(2):
                for half in range(2):
                    spot = half * 4 + face
                    code = spread(codes[turn, pl.ds(group * 8 + spot, 1), :])
                    far = code >= LANES
                    lane = code & (LANES - 1)
                    for comp in range(4):
                        row = ((turn * BLOCKS + group * 2 + half) * 4 + face) * 32 + comp * 8
                        there = pick(came[pl.ds(face * 32 + comp * 8, 8), :], lane)
                        near[pl.ds((turn * 4 + comp) * 64 + spot * 8, 8), :] = jnp.where(
                            far, there, found[rows_of(row, 8), :]
                        )
                    marks.append(0.0 * there)
                    yield

    def settle(group, near, marks):
        eight = pl.ds(pl.multiple_of(group * 8, 8), 8)
        kind = rows_kind[eight, :]
        factor = rows_factor[eight, :]
        coarse, lower, upper = kind == 3, kind == 1, kind == 2
        left, right, high = [], [], []
        for comp in range(4):
            own = [
                traces[pl.ds(group * 256 + comp * 8 + node, 8, stride=32), :] for node in range(8)
            ]
            other = [near[pl.ds(comp * 64 + node, 8, stride=8), :] for node in range(8)]
            blend = [jnp.where(coarse, own[n], other[n]) for n in range(8)]
            even = [blend[b] + blend[7 - b] for b in range(4)]
            odd = [blend[b] - blend[7 - b] for b in range(4)]
            low_of, high_of = [None] * 8, [None] * 8
            for a in range(8):
                one, two = weighted(FOLD_EVEN[a], even), weighted(FOLD_ODD[a], odd)
                low_of[a] = one + two
                high_of[7 - a] = one - two
                if a % 2:
                    yield
            left.append([jnp.where(coarse, low_of[n], own[n]) for n in range(8)])
            right.append(
                [jnp.where(lower, low_of[n], jnp.where(upper, high_of[n], other[n])) for n in range(8)]
            )
            high.append(high_of)
        one, two = [], []
        for node in range(8):
            above = [near[pl.ds((4 + comp) * 64 + node, 8, stride=8), :] for comp in range(4)]
            sign = quarter
            while marks:
                sign = sign + marks.pop(0)
            one.append(numeric_flux([v[node] for v in left], [v[node] for v in right], sign))
            two.append(numeric_flux([v[node] for v in high], above, sign))
            yield
        for comp in range(3):
            total = [one[b][comp] + two[7 - b][comp] for b in range(8)]
            differ = [one[b][comp] - two[7 - b][comp] for b in range(8)]
            for a in range(4):
                same, anti = weighted(JOIN_SUM[a], total), weighted(JOIN_DIFF[a], differ)
                for node, joined in ((a, same + anti), (7 - a, same - anti)):
                    changes[pl.ds(comp * 64 + node, 8, stride=8), :] = factor * jnp.where(
                        coarse, joined, one[node][comp]
                    )
        for half in range(2):
            into = pl.multiple_of((group * 2 + half) * MOVED, MOVED)
            for face in range(FACES):
                for comp in range(3):
                    rows = face_rows(into + component(face, comp) * 64, face)
                    moved[rows, :] = (
                        moved[rows, :] - changes[pl.ds(comp * 64 + (half * 4 + face) * 8, 8), :]
                    )
            for copy in copies(group * 2 + half):
                copy.start()

    def both(next_group, into, group, held):
        marks = []
        interleave(fetch(next_group, into, marks), settle(group, held, marks))

    def body(step, carry):
        both(2 * step + 1, near_b, 2 * step, near_a)
        both(2 * step + 2, near_a, 2 * step + 1, near_b)
        return carry

    interleave(fetch(0, near_a, []))
    lax.fori_loop(0, GROUPS // 2, body, 0)
    interleave(settle(GROUPS - 1, near_a, []))

    def finish(block, carry):
        for copy in copies(block):
            copy.wait()
        return carry

    lax.fori_loop(0, BLOCKS, finish, 0)


VM = pl.BlockSpec(memory_space=pltpu.VMEM)
FAR = pl.BlockSpec(memory_space=pltpu.HBM)
ANY = pl.BlockSpec(memory_space=pl.ANY)
PARAMS = pltpu.CompilerParams(vmem_limit_bytes=24 * 1024 * 1024)


def swap(block, axis, phase):
    size = lax.axis_size(axis)
    route = [(i, (((i + phase) ^ 1) - phase) % size) for i in range(size)]
    return lax.ppermute(block, axis, route)


def placed(memory, *arrays):
    return [pltpu.with_memory_space_constraint(array, memory) for array in arrays]


def on_device(depth, momentum, bed, levels, kinds, send, trace_src, back, mortar_src):
    depth = depth.reshape(64, ELEMS)
    momentum = momentum.reshape(128, ELEMS)
    bed = bed.reshape(64, ELEMS)
    message = pltpu.VMEM((32, LANES), F32)
    tables = (
        pltpu.VMEM((4, ELEMS), I32),
        pltpu.VMEM((4, ELEMS), I32),
        pltpu.VMEM((2, 4, ELEMS), I32),
        pltpu.VMEM((ELEMS,), I32),
    )
    done = (
        pltpu.VMEM((BLOCKS * MOVED, LANES), F32),
        pltpu.VMEM((2 * BLOCKS * 128, LANES), F32),
        pltpu.VMEM((2, 4 * BLOCKS, LANES), I32),
        pltpu.VMEM((4 * BLOCKS, LANES), I32),
        pltpu.VMEM((4 * BLOCKS, LANES), F32),
    )
    held = pltpu.VMEM((BLOCKS * STATE, LANES), F32), pltpu.VMEM((BLOCKS * TRACE, LANES), F32)
    work_space = [pltpu.VMEM((128, LANES), F32), pltpu.VMEM((16, LANES), I32)]
    packed = pl.pallas_call(
        pack_kernel,
        out_shape=held + (message,) * 4 + tables + done,
        in_specs=[FAR] * 9,
        out_specs=[VM] * 15,
        scratch_shapes=work_space
        + [
            pltpu.VMEM((144,), I32),
            pltpu.VMEM((96,), I32),
            pltpu.SemaphoreType.DMA((3, BLOCKS)),
            pltpu.SemaphoreType.DMA((6,)),
        ],
        compiler_params=PARAMS,
        name="pack",
    )(*placed(pltpu.HBM, depth, momentum, bed, send, back, kinds, trace_src, mortar_src, levels))
    state, traces = packed[:2]
    wide_a, narrow_b, narrow_a, wide_b = packed[2:6]
    got_wb = swap(wide_b, "wide", 1)
    got_na = swap(narrow_a, "narrow", 0)
    got_nb = swap(narrow_b, "narrow", 1)
    got_wa = swap(wide_a, "wide", 0)
    moved, found, codes, rows_kind, rows_factor = pl.pallas_call(
        interior_kernel,
        out_shape=done,
        in_specs=[VM] * 11,
        out_specs=[VM] * 5,
        input_output_aliases={6 + i: i for i in range(5)},
        scratch_shapes=work_space,
        compiler_params=PARAMS,
        name="interior",
        cost_estimate=pl.CostEstimate(flops=20_000_000, bytes_accessed=2_000_000, transcendentals=0),
    )(*placed(pltpu.VMEM, state, traces, *packed[6:15]))
    new_depth, new_moment, _ = pl.pallas_call(
        surface_kernel,
        out_shape=(
            jax.ShapeDtypeStruct((64, ELEMS), F32),
            jax.ShapeDtypeStruct((128, ELEMS), F32),
            pltpu.VMEM((BLOCKS * MOVED, LANES), F32),
        ),
        in_specs=[VM] * 10,
        out_specs=[ANY, ANY, VM],
        input_output_aliases={0: 2},
        scratch_shapes=[
            pltpu.VMEM((128, LANES), F32),
            pltpu.VMEM((512, LANES), F32),
            pltpu.VMEM((512, LANES), F32),
            pltpu.VMEM((192, LANES), F32),
            pltpu.SemaphoreType.DMA((2, BLOCKS)),
        ],
        compiler_params=PARAMS,
        name="surface",
    )(
        *placed(
            pltpu.VMEM, moved, traces, found, codes, rows_kind, rows_factor, got_wa, got_nb, got_na, got_wb
        )
    )
    return new_depth.reshape(8, 8, ELEMS), new_moment.reshape(2, 8, 8, ELEMS)


def solution(mesh):
    both = ("wide", "narrow")
    placed = (
        P(None, None, both),
        P(None, None, None, both),
        P(None, None, both),
        P(both),
        P(None, both),
        P(both),
        P(None, both),
        P(both),
        P(None, None, both),
    )
    return jax.shard_map(
        on_device,
        mesh=mesh,
        in_specs=placed,
        out_specs=(P(None, None, both), P(None, None, None, both)),
        check_vma=False,
    )
```

```python
import jax
import jax.numpy as jnp
import numpy as np
from jax import lax
from jax.experimental import pallas as pl
from jax.experimental.pallas import tpu as pltpu
from jax.sharding import PartitionSpec as P

NODES = 8
ELEMS = 1280
LANES = 128
AHEAD = 35
PER_BLOCK = 5
FIRST_MORE = 1
BLOCKS = ELEMS // LANES
TREE_BLOCKS = BLOCKS // 2
GROUPS = BLOCKS // 2
FACES = 4
STATE, TRACE, MOVED = 256, 128, 192
LOCAL = FACES * ELEMS
STEP = 0.005
F32 = jnp.float32
I32 = jnp.int32

SEND_AT = (0, 48, 96, 120)
SEND_CAP = (48, 48, 24, 24)
BACK_AT = (48, 96, 64, 80)
BACK_CAP = (32, 32, 16, 16)
RECV_OFF = (0, 48, 96, 120)
RECV_LANE = (48, 0, 120, 96)
RETN_OFF = (0, 32, 64, 80)
RETN_LANE = (96, 48, 80, 64)


def tables():
    degree = NODES - 1

    def legendre(points):
        before, current = np.ones(points.shape), points * 1.0
        for order in range(2, degree + 1):
            before, current = (
                current,
                ((2.0 * order - 1.0) * points * current - (order - 1.0) * before) / order,
            )
        return current, before

    points = -np.cos(np.pi * np.arange(NODES) / degree)
    for _ in range(100):
        top, below = legendre(points)
        points = points - (points * top - below) / (NODES * top)
    points[0], points[-1] = -1.0, 1.0
    values = legendre(points)[0]
    weights = 2.0 / (degree * NODES * values * values)
    deriv = np.zeros((NODES, NODES))
    for i in range(NODES):
        for k in range(NODES):
            if i != k:
                deriv[i, k] = values[i] / (values[k] * (points[i] - points[k]))

    def lagrange(targets):
        table = np.ones((NODES, NODES))
        for k in range(NODES):
            for o in range(NODES):
                if o != k:
                    table[:, k] = table[:, k] * (targets - points[o]) / (points[k] - points[o])
        return table

    low, high = lagrange((points - 1.0) / 2.0), lagrange((points + 1.0) / 2.0)
    proj_low = 0.5 * low.T * weights[None, :] / weights[:, None]
    proj_high = 0.5 * high.T * weights[None, :] / weights[:, None]
    return weights, deriv, low, high, proj_low, proj_high


WEIGHTS, DERIV, INTERP_LOW, INTERP_HIGH, PROJ_LOW, PROJ_HIGH = tables()
SKEW = WEIGHTS[:, None] * DERIV
LIFT = 1.0 / WEIGHTS[0]


FOLD_EVEN = 0.5 * (INTERP_LOW + INTERP_LOW[:, ::-1])[:, :4]
FOLD_ODD = 0.5 * (INTERP_LOW - INTERP_LOW[:, ::-1])[:, :4]
JOIN_SUM = 0.5 * (PROJ_LOW + PROJ_LOW[::-1])[:4]
JOIN_DIFF = 0.5 * (PROJ_LOW - PROJ_LOW[::-1])[:4]


def face_rows(base, face):
    if face == 0:
        return pl.ds(base, 8)
    if face == 1:
        return pl.ds(base + 56, 8)
    if face == 2:
        return pl.ds(base, 8, stride=8)
    return pl.ds(base + 7, 8, stride=8)


def trace_row(block, face, comp):
    return (block // 2) * 256 + comp * 64 + ((block % 2) * 4 + face) * 8


def component(face, place):
    return place if face < 2 or place in (0, 3) else 3 - place


def lanes_of(block):
    return pl.ds(pl.multiple_of(block * LANES, LANES), LANES)


def rows_of(base, count):
    return pl.ds(pl.multiple_of(base, 8), count)


def spread(row):
    return jnp.broadcast_to(row, (8, LANES))


def pick(source, lane):
    return jnp.take_along_axis(source, lane, axis=1, mode="promise_in_bounds")


def pack_kernel(
    depth, moment, bed, send, back, kinds_far, trace_far, mortar_far, levels_far,
    state, traces, wide_a, narrow_b, narrow_a, wide_b, kinds, trace_src, mortar_src, levels,
    *rest
):
    out_refs, scratch = rest[:5], rest[5:7]
    send_list, back_list, sems, list_sems = rest[7:]
    list_copies = [
        pltpu.make_async_copy(send, send_list, list_sems.at[0]),
        pltpu.make_async_copy(back, back_list, list_sems.at[1]),
    ]
    for copy in list_copies:
        copy.start()
    copies = []
    table_copies = [
        pltpu.make_async_copy(kinds_far, kinds, list_sems.at[2]),
        pltpu.make_async_copy(trace_far, trace_src, list_sems.at[3]),
        pltpu.make_async_copy(mortar_far, mortar_src, list_sems.at[4]),
        pltpu.make_async_copy(levels_far, levels, list_sems.at[5]),
    ]
    for block in range(BLOCKS):
        lanes = pl.ds(block * LANES, LANES)
        base = block * STATE
        for slot, (source, row, count) in enumerate(
            ((depth, 0, 64), (moment, 64, 128), (bed, 192, 64))
        ):
            copy = pltpu.make_async_copy(
                source.at[:, lanes], state.at[pl.ds(base + row, count)], sems.at[slot, block]
            )
            copy.start()
            copies.append(copy)
    for copy in table_copies:
        copy.start()
    for copy in list_copies:
        copy.wait()
    lane_id = lax.broadcasted_iota(I32, (8, LANES), 1)
    def full(row):
        row = row.reshape(1, row.shape[0])
        return spread(jnp.concatenate([row, jnp.zeros((1, LANES - row.shape[1]), I32)], axis=1))

    send_first = spread(send_list[pl.ds(0, LANES)].reshape(1, LANES))
    send_last = full(send_list[pl.ds(LANES, 16)])
    back_row = full(back_list[...])
    backs = (pltpu.roll(back_row, 48, 1), pltpu.roll(back_row, 64, 1), back_row, back_row)
    index = []
    for way in range(4):
        row = send_first
        if way == 3:
            row = jnp.where(lane_id < 64, send_last, send_first)
        inside = (lane_id >= BACK_AT[way]) & (lane_id < BACK_AT[way] + BACK_CAP[way])
        row = jnp.where(inside, backs[way], row)
        index.append(row - way * ELEMS)
    out = [[jnp.zeros((8, LANES), F32) for _ in range(4)] for _ in range(4)]
    lane = [row & (LANES - 1) for row in index]
    place = [row >> 7 for row in index]
    for block in range(BLOCKS):
        for copy in copies[3 * block : 3 * block + 3]:
            copy.wait()
        for face in range(FACES):
            for comp in range(4):
                piece = state[face_rows(block * STATE + component(face, comp) * 64, face), :]
                if comp == 0:
                    height = piece
                elif comp == 3:
                    piece = piece + height
                traces[pl.ds(trace_row(block, face, comp), 8), :] = piece
    for way in range(4):
        for block in range(BLOCKS):
            here = place[way] == block
            for comp in range(4):
                got = pick(traces[pl.ds(trace_row(block, way, comp), 8), :], lane[way])
                out[way][comp] = got if block == 0 else jnp.where(here, got, out[way][comp])
    wide_even = (lax.axis_index("wide") & 1) == 0
    narrow_even = (lax.axis_index("narrow") & 1) == 0
    for comp in range(4):
        rows = pl.ds(comp * 8, 8)
        wide_a[rows, :] = jnp.where(wide_even, out[1][comp], out[0][comp])
        wide_b[rows, :] = jnp.where(wide_even, out[0][comp], out[1][comp])
        narrow_a[rows, :] = jnp.where(narrow_even, out[3][comp], out[2][comp])
        narrow_b[rows, :] = jnp.where(narrow_even, out[2][comp], out[3][comp])
    for copy in table_copies:
        copy.wait()
    work = block_worker(state, traces, kinds, trace_src, mortar_src, levels, out_refs, scratch)

    work_through(work, 0, blocks_ahead())


def line_terms(height, normal, tangent, bed, marks):
    def accumulate(slot, i, value, minus=False):
        if slot[i] is None:
            slot[i] = -value if minus else value
        else:
            slot[i] = slot[i] - value if minus else slot[i] + value

    slope = [None] * 8
    for i in range(8):
        for k in range(i + 1, 8):
            bump = float(SKEW[i, k]) * (bed[k] - bed[i])
            accumulate(slope, i, bump)
            accumulate(slope, k, bump)
        yield
    square = [2.0 * (h * h) for h in height]
    mass = [None] * 8
    along = [(4.0 * height[i]) * slope[i] for i in range(8)]
    cross = [None] * 8
    for i in range(8):
        for k in range(i + 1, 8):
            q = float(SKEW[i, k])
            un = normal[i] + normal[k]
            if marks:
                un = un + marks.pop(0)
            first = (q * (height[i] + height[k])) * un
            second = first * un + q * (square[i] + square[k])
            third = first * (tangent[i] + tangent[k])
            for slot, value in ((mass, first), (along, second), (cross, third)):
                accumulate(slot, i, value)
                accumulate(slot, k, value, True)
            yield
    out = []
    for i in range(8):
        scale = STEP / WEIGHTS[i]
        out.append(
            (float(0.5 * scale) * mass[i], float(0.25 * scale) * along[i], float(0.25 * scale) * cross[i])
        )
    return out


def volume_of(state, moved, speeds, base, into, metric, marks):
    def rows(comp, j, across):
        if across:
            return pl.ds(comp * 64 + j, 8, stride=8)
        return pl.ds(comp * 64 + j * 8, 8)

    def at(start, window):
        return pl.ds(start + window.start, window.size, window.stride)

    height = [state[at(base, rows(0, j, False)), :] for j in range(8)]
    bed = [state[at(base, rows(3, j, False)), :] for j in range(8)]
    vel_x, vel_y = [], []
    for j in range(8):
        inverse = 1.0 / height[j]
        vel_x.append(state[at(base, rows(1, j, False)), :] * inverse)
        vel_y.append(state[at(base, rows(2, j, False)), :] * inverse)
        speeds[rows(0, j, False), :] = vel_x[j]
        speeds[rows(1, j, False), :] = vel_y[j]
    terms = yield from line_terms(height, vel_x, vel_y, bed, marks)
    for i in range(8):
        for comp, value in enumerate(terms[i]):
            moved[at(into, rows(comp, i, False)), :] = (
                state[at(base, rows(comp, i, False)), :] - metric * value
            )
    height = [state[at(base, rows(0, j, True)), :] for j in range(8)]
    bed = [state[at(base, rows(3, j, True)), :] for j in range(8)]
    vel_x = [speeds[rows(0, j, True), :] for j in range(8)]
    vel_y = [speeds[rows(1, j, True), :] for j in range(8)]
    terms = yield from line_terms(height, vel_y, vel_x, bed, marks)
    for j in range(8):
        mass, along, cross = terms[j]
        for comp, value in enumerate((mass, cross, along)):
            window = at(into, rows(comp, j, True))
            moved[window, :] = moved[window, :] - metric * value


def gather_of(traces, found, picks, block, tree, marks):
    for face in range(FACES):
        own = range(tree * TREE_BLOCKS, (tree + 1) * TREE_BLOCKS)
        reach = range(BLOCKS) if face == 3 - tree else own
        for turn in range(2):
            lane = spread(picks[pl.ds(turn * 8 + face, 1), :])
            place = spread(picks[pl.ds(turn * 8 + 4 + face, 1), :])
            total = [None] * 4
            for other in reach:
                here = place == other
                for comp in range(4):
                    got = pick(traces[pl.ds(trace_row(other, face ^ 1, comp), 8), :], lane)
                    total[comp] = got if total[comp] is None else jnp.where(here, got, total[comp])
                yield
            for comp in range(4):
                row = ((turn * BLOCKS + block) * 4 + face) * 32 + comp * 8
                found[rows_of(row, 8), :] = total[comp]
            marks.append(0.0 * total[3])


def interleave(*works):
    works = list(works)
    while works:
        for work in list(works):
            if next(work, works) is works:
                works.remove(work)


def block_worker(state, traces, kinds, trace_src, mortar_src, levels, out, scratch):
    moved, found, codes, rows_kind, rows_factor = out
    speeds, picks = scratch
    face_id = lax.broadcasted_iota(I32, (4, LANES), 0)

    def by_face(values):
        total = jnp.full((4, LANES), values[3], I32)
        for face in range(3):
            total = jnp.where(face_id == face, values[face], total)
        return total

    home = by_face([-(face ^ 1) * ELEMS for face in range(FACES)])
    recv_shift = by_face([RECV_LANE[f] - RECV_OFF[f] - LOCAL for f in range(FACES)])
    retn_shift = by_face([RETN_LANE[f] - RETN_OFF[f] - LOCAL for f in range(FACES)])

    def work(block, tree):
        lanes = lanes_of(block)
        base = pl.multiple_of(block * STATE, STATE)
        into = pl.multiple_of(block * MOVED, MOVED)
        level_row = (levels[lanes].reshape(1, LANES) + 1).astype(F32)
        kind = kinds[:, lanes]
        coarse = kind == 3
        first = jnp.where(coarse, mortar_src[0, :, lanes], trace_src[:, lanes])
        second = mortar_src[1, :, lanes]
        four = pl.ds(pl.multiple_of(block * 4, 4), 4)
        for turn, (index, shift) in enumerate(
            ((first, jnp.where(coarse, retn_shift, recv_shift)), (second, retn_shift))
        ):
            far = index >= LOCAL
            index = index + jnp.where(far, shift, home)
            lane = index & (LANES - 1)
            picks[pl.ds(turn * 8, 4), :] = lane
            picks[pl.ds(turn * 8 + 4, 4), :] = jnp.where(far, BLOCKS, index >> 7)
            codes[turn, four, :] = jnp.where(far, lane + LANES, lane)
        rows_kind[four, :] = kind
        rows_factor[four, :] = jnp.broadcast_to(level_row * float(0.5 * LIFT * STEP), (4, LANES))
        marks = []
        interleave(
            gather_of(traces, found, picks, block, tree, marks),
            volume_of(state, moved, speeds, base, into, spread(level_row), marks),
        )

    return work


def work_through(work, start, stop):
    for tree in range(2):

        def step(block, carry, tree=tree):
            work(block, tree)
            return carry

        low, high = tree * TREE_BLOCKS, (tree + 1) * TREE_BLOCKS
        lax.fori_loop(jnp.maximum(start, low), jnp.minimum(stop, high), step, 0)


def blocks_ahead():
    wide, narrow = lax.axis_index("wide"), lax.axis_index("narrow")
    x, z, core = wide >> 3, (wide >> 1) & 3, wide & 1

    def one_of(at, values):
        total = jnp.int32(values[3])
        for i in range(3):
            total = jnp.where(at == i, jnp.int32(values[i]), total)
        return total

    lead = AHEAD - one_of(narrow, (0, 0, 28, 35)) - one_of(x, (0, 10, 12, 14)) - one_of(z, (0, 10, 22, 26))
    ahead = jnp.clip((lead + 5 * core) // PER_BLOCK, 0, TREE_BLOCKS)
    return ahead + jnp.where((wide == 0) & (narrow < 2), FIRST_MORE, 0)


def interior_kernel(
    state, traces, kinds, trace_src, mortar_src, levels, *rest
):
    out, scratch = rest[5:10], rest[10:]
    work = block_worker(state, traces, kinds, trace_src, mortar_src, levels, out, scratch)

    work_through(work, blocks_ahead(), BLOCKS)


def numeric_flux(left, right, sign):
    inv_l, inv_r = 1.0 / left[0], 1.0 / right[0]
    un_l, un_r = left[1] * inv_l, right[1] * inv_r
    un = un_l + un_r
    ut = left[2] * inv_l + right[2] * inv_r
    speed = jnp.maximum(
        jnp.abs(un_l) + left[0] * lax.rsqrt(left[0]), jnp.abs(un_r) + right[0] * lax.rsqrt(right[0])
    )
    first = (sign * (left[0] + right[0])) * un
    middle = 0.5 * first
    second = middle * un + sign * (left[0] * left[0] + right[0] * right[0])
    third = middle * ut
    return (
        first - speed * (right[3] - left[3]),
        second - speed * (right[1] - left[1]),
        third - speed * (right[2] - left[2]),
    )


def weighted(coefficients, values):
    total = None
    for coefficient, value in zip(coefficients, values):
        if abs(coefficient) > 1e-12:
            term = float(coefficient) * value
            total = term if total is None else total + term
    return total


def weighted(coefficients, values):
    total = None
    for coefficient, value in zip(coefficients, values):
        term = float(coefficient) * value
        total = term if total is None else total + term
    return total


def surface_kernel(
    moved_in, traces, found, codes, rows_kind, rows_factor, got_wa, got_nb, got_na, got_wb,
    new_depth, new_moment, moved, came, near_a, near_b, changes, sems
):
    del moved_in
    wide_even = (lax.axis_index("wide") & 1) == 0
    narrow_even = (lax.axis_index("narrow") & 1) == 0
    for comp in range(4):
        rows = pl.ds(comp * 8, 8)
        wide = got_wa[rows, :], got_wb[rows, :]
        narrow = got_na[rows, :], got_nb[rows, :]
        came[pl.ds(comp * 8, 8), :] = jnp.where(wide_even, wide[1], wide[0])
        came[pl.ds(32 + comp * 8, 8), :] = jnp.where(wide_even, wide[0], wide[1])
        came[pl.ds(64 + comp * 8, 8), :] = jnp.where(narrow_even, narrow[1], narrow[0])
        came[pl.ds(96 + comp * 8, 8), :] = jnp.where(narrow_even, narrow[0], narrow[1])
    row_id = lax.broadcasted_iota(I32, (8, LANES), 0)
    normal_half = jnp.where((row_id & 1) == 1, 0.5, -0.5).astype(F32)

    def copies(block):
        lanes = lanes_of(block)
        row = pl.multiple_of(block * MOVED, MOVED)
        return (
            pltpu.make_async_copy(moved.at[pl.ds(row, 64)], new_depth.at[:, lanes], sems.at[0, block]),
            pltpu.make_async_copy(
                moved.at[pl.ds(row + 64, 128)], new_moment.at[:, lanes], sems.at[1, block]
            ),
        )

    def fetch(group, near, marks):
        for face in range(FACES):
            for turn in range(2):
                for half in range(2):
                    spot = half * 4 + face
                    code = spread(codes[turn, pl.ds(group * 8 + spot, 1), :])
                    far = code >= LANES
                    lane = code & (LANES - 1)
                    for comp in range(4):
                        row = ((turn * BLOCKS + group * 2 + half) * 4 + face) * 32 + comp * 8
                        there = pick(came[pl.ds(face * 32 + comp * 8, 8), :], lane)
                        near[pl.ds((turn * 4 + comp) * 64 + spot * 8, 8), :] = jnp.where(
                            far, there, found[rows_of(row, 8), :]
                        )
                    marks.append(0.0 * there)
                    yield

    def settle(group, near, marks):
        eight = pl.ds(pl.multiple_of(group * 8, 8), 8)
        kind = rows_kind[eight, :]
        factor = rows_factor[eight, :]
        coarse, lower, upper = kind == 3, kind == 1, kind == 2
        left, right, high = [], [], []
        for comp in range(4):
            own = [
                traces[pl.ds(group * 256 + comp * 64 + node, 8, stride=8), :] for node in range(8)
            ]
            other = [near[pl.ds(comp * 64 + node, 8, stride=8), :] for node in range(8)]
            blend = [jnp.where(coarse, own[n], other[n]) for n in range(8)]
            even = [blend[b] + blend[7 - b] for b in range(4)]
            odd = [blend[b] - blend[7 - b] for b in range(4)]
            low_of, high_of = [None] * 8, [None] * 8
            for a in range(8):
                one, two = weighted(FOLD_EVEN[a], even), weighted(FOLD_ODD[a], odd)
                if a == 0:
                    low_of[0], high_of[7] = blend[0], blend[7]
                elif two is None:
                    low_of[a] = high_of[7 - a] = one
                else:
                    low_of[a], high_of[7 - a] = one + two, one - two
                if a % 2:
                    yield
            left.append([jnp.where(coarse, low_of[n], own[n]) for n in range(8)])
            right.append(
                [jnp.where(lower, low_of[n], jnp.where(upper, high_of[n], other[n])) for n in range(8)]
            )
            high.append(high_of)
        one, two = [], []
        for node in range(8):
            above = [near[pl.ds((4 + comp) * 64 + node, 8, stride=8), :] for comp in range(4)]
            sign = normal_half
            while marks:
                sign = sign + marks.pop(0)
            one.append(numeric_flux([v[node] for v in left], [v[node] for v in right], sign))
            two.append(numeric_flux([v[node] for v in high], above, sign))
            yield
        for comp in range(3):
            total = [one[b][comp] + two[7 - b][comp] for b in range(8)]
            differ = [one[b][comp] - two[7 - b][comp] for b in range(8)]
            for a in range(4):
                same, anti = weighted(JOIN_SUM[a], total), weighted(JOIN_DIFF[a], differ)
                for node, joined in ((a, same + anti), (7 - a, same - anti)):
                    changes[pl.ds(comp * 64 + node, 8, stride=8), :] = factor * jnp.where(
                        coarse, joined, one[node][comp]
                    )
        for half in range(2):
            into = pl.multiple_of((group * 2 + half) * MOVED, MOVED)
            for face in range(FACES):
                for comp in range(3):
                    rows = face_rows(into + component(face, comp) * 64, face)
                    moved[rows, :] = (
                        moved[rows, :] - changes[pl.ds(comp * 64 + (half * 4 + face) * 8, 8), :]
                    )
            for copy in copies(group * 2 + half):
                copy.start()

    def both(next_group, into, group, held):
        marks = []
        interleave(fetch(next_group, into, marks), settle(group, held, marks))

    def body(step, carry):
        both(2 * step + 1, near_b, 2 * step, near_a)
        both(2 * step + 2, near_a, 2 * step + 1, near_b)
        return carry

    interleave(fetch(0, near_a, []))
    lax.fori_loop(0, GROUPS // 2, body, 0)
    interleave(settle(GROUPS - 1, near_a, []))

    def finish(block, carry):
        for copy in copies(block):
            copy.wait()
        return carry

    lax.fori_loop(0, BLOCKS, finish, 0)


VM = pl.BlockSpec(memory_space=pltpu.VMEM)
FAR = pl.BlockSpec(memory_space=pltpu.HBM)
ANY = pl.BlockSpec(memory_space=pl.ANY)
PARAMS = pltpu.CompilerParams(vmem_limit_bytes=24 * 1024 * 1024)


def swap(block, axis, phase):
    size = lax.axis_size(axis)
    route = [(i, (((i + phase) ^ 1) - phase) % size) for i in range(size)]
    return lax.ppermute(block, axis, route)


def placed(memory, *arrays):
    return [pltpu.with_memory_space_constraint(array, memory) for array in arrays]


def on_device(depth, momentum, bed, levels, kinds, send, trace_src, back, mortar_src):
    depth = depth.reshape(64, ELEMS)
    momentum = momentum.reshape(128, ELEMS)
    bed = bed.reshape(64, ELEMS)
    message = pltpu.VMEM((32, LANES), F32)
    tables = (
        pltpu.VMEM((4, ELEMS), I32),
        pltpu.VMEM((4, ELEMS), I32),
        pltpu.VMEM((2, 4, ELEMS), I32),
        pltpu.VMEM((ELEMS,), I32),
    )
    done = (
        pltpu.VMEM((BLOCKS * MOVED, LANES), F32),
        pltpu.VMEM((2 * BLOCKS * 128, LANES), F32),
        pltpu.VMEM((2, 4 * BLOCKS, LANES), I32),
        pltpu.VMEM((4 * BLOCKS, LANES), I32),
        pltpu.VMEM((4 * BLOCKS, LANES), F32),
    )
    held = pltpu.VMEM((BLOCKS * STATE, LANES), F32), pltpu.VMEM((BLOCKS * TRACE, LANES), F32)
    work_space = [pltpu.VMEM((128, LANES), F32), pltpu.VMEM((16, LANES), I32)]
    packed = pl.pallas_call(
        pack_kernel,
        out_shape=held + (message,) * 4 + tables + done,
        in_specs=[FAR] * 9,
        out_specs=[VM] * 15,
        scratch_shapes=work_space
        + [
            pltpu.VMEM((144,), I32),
            pltpu.VMEM((96,), I32),
            pltpu.SemaphoreType.DMA((3, BLOCKS)),
            pltpu.SemaphoreType.DMA((6,)),
        ],
        compiler_params=PARAMS,
        name="pack",
    )(*placed(pltpu.HBM, depth, momentum, bed, send, back, kinds, trace_src, mortar_src, levels))
    state, traces = packed[:2]
    wide_a, narrow_b, narrow_a, wide_b = packed[2:6]
    got_wb = swap(wide_b, "wide", 1)
    got_na = swap(narrow_a, "narrow", 0)
    got_nb = swap(narrow_b, "narrow", 1)
    got_wa = swap(wide_a, "wide", 0)
    moved, found, codes, rows_kind, rows_factor = pl.pallas_call(
        interior_kernel,
        out_shape=done,
        in_specs=[VM] * 11,
        out_specs=[VM] * 5,
        input_output_aliases={6 + i: i for i in range(5)},
        scratch_shapes=work_space,
        compiler_params=PARAMS,
        name="interior",
        cost_estimate=pl.CostEstimate(flops=20_000_000, bytes_accessed=2_000_000, transcendentals=0),
    )(*placed(pltpu.VMEM, state, traces, *packed[6:15]))
    new_depth, new_moment, _ = pl.pallas_call(
        surface_kernel,
        out_shape=(
            jax.ShapeDtypeStruct((64, ELEMS), F32),
            jax.ShapeDtypeStruct((128, ELEMS), F32),
            pltpu.VMEM((BLOCKS * MOVED, LANES), F32),
        ),
        in_specs=[VM] * 10,
        out_specs=[ANY, ANY, VM],
        input_output_aliases={0: 2},
        scratch_shapes=[
            pltpu.VMEM((128, LANES), F32),
            pltpu.VMEM((512, LANES), F32),
            pltpu.VMEM((512, LANES), F32),
            pltpu.VMEM((192, LANES), F32),
            pltpu.SemaphoreType.DMA((2, BLOCKS)),
        ],
        compiler_params=PARAMS,
        name="surface",
    )(
        *placed(
            pltpu.VMEM, moved, traces, found, codes, rows_kind, rows_factor, got_wa, got_nb, got_na, got_wb
        )
    )
    return new_depth.reshape(8, 8, ELEMS), new_moment.reshape(2, 8, 8, ELEMS)


def solution(mesh):
    both = ("wide", "narrow")
    placed = (
        P(None, None, both),
        P(None, None, None, both),
        P(None, None, both),
        P(both),
        P(None, both),
        P(both),
        P(None, both),
        P(both),
        P(None, None, both),
    )
    return jax.shard_map(
        on_device,
        mesh=mesh,
        in_specs=placed,
        out_specs=(P(None, None, both), P(None, None, None, both)),
        check_vma=False,
    )
```

```python
import jax
import jax.numpy as jnp
import numpy as np
from jax import lax
from jax.experimental import pallas as pl
from jax.experimental.pallas import tpu as pltpu
from jax.sharding import PartitionSpec as P

NODES = 8
ELEMS = 1280
LANES = 128
AHEAD = 35
PER_BLOCK = 5
FIRST_MORE = 1
BLOCKS = ELEMS // LANES
TREE_BLOCKS = BLOCKS // 2
GROUPS = BLOCKS // 2
FACES = 4
STATE, TRACE, MOVED = 256, 128, 192
LOCAL = FACES * ELEMS
STEP = 0.005
F32 = jnp.float32
I32 = jnp.int32

SEND_AT = (0, 48, 96, 120)
SEND_CAP = (48, 48, 24, 24)
BACK_AT = (48, 96, 64, 80)
BACK_CAP = (32, 32, 16, 16)
RECV_OFF = (0, 48, 96, 120)
RECV_LANE = (48, 0, 120, 96)
RETN_OFF = (0, 32, 64, 80)
RETN_LANE = (96, 48, 80, 64)


def tables():
    degree = NODES - 1

    def legendre(points):
        before, current = np.ones(points.shape), points * 1.0
        for order in range(2, degree + 1):
            before, current = (
                current,
                ((2.0 * order - 1.0) * points * current - (order - 1.0) * before) / order,
            )
        return current, before

    points = -np.cos(np.pi * np.arange(NODES) / degree)
    for _ in range(100):
        top, below = legendre(points)
        points = points - (points * top - below) / (NODES * top)
    points[0], points[-1] = -1.0, 1.0
    values = legendre(points)[0]
    weights = 2.0 / (degree * NODES * values * values)
    deriv = np.zeros((NODES, NODES))
    for i in range(NODES):
        for k in range(NODES):
            if i != k:
                deriv[i, k] = values[i] / (values[k] * (points[i] - points[k]))

    def lagrange(targets):
        table = np.ones((NODES, NODES))
        for k in range(NODES):
            for o in range(NODES):
                if o != k:
                    table[:, k] = table[:, k] * (targets - points[o]) / (points[k] - points[o])
        return table

    low, high = lagrange((points - 1.0) / 2.0), lagrange((points + 1.0) / 2.0)
    proj_low = 0.5 * low.T * weights[None, :] / weights[:, None]
    proj_high = 0.5 * high.T * weights[None, :] / weights[:, None]
    return weights, deriv, low, high, proj_low, proj_high


WEIGHTS, DERIV, INTERP_LOW, INTERP_HIGH, PROJ_LOW, PROJ_HIGH = tables()
SKEW = WEIGHTS[:, None] * DERIV
LIFT = 1.0 / WEIGHTS[0]


FOLD_EVEN = 0.5 * (INTERP_LOW + INTERP_LOW[:, ::-1])[:, :4]
FOLD_ODD = 0.5 * (INTERP_LOW - INTERP_LOW[:, ::-1])[:, :4]
JOIN_SUM = 0.5 * (PROJ_LOW + PROJ_LOW[::-1])[:4]
JOIN_DIFF = 0.5 * (PROJ_LOW - PROJ_LOW[::-1])[:4]


def face_rows(base, face):
    if face == 0:
        return pl.ds(base, 8)
    if face == 1:
        return pl.ds(base + 56, 8)
    if face == 2:
        return pl.ds(base, 8, stride=8)
    return pl.ds(base + 7, 8, stride=8)


def trace_row(block, face, comp):
    return (block // 2) * 256 + comp * 64 + ((block % 2) * 4 + face) * 8


def component(face, place):
    return place if face < 2 or place in (0, 3) else 3 - place


def lanes_of(block):
    return pl.ds(pl.multiple_of(block * LANES, LANES), LANES)


def rows_of(base, count):
    return pl.ds(pl.multiple_of(base, 8), count)


def spread(row):
    return jnp.broadcast_to(row, (8, LANES))


def pick(source, lane):
    return jnp.take_along_axis(source, lane, axis=1, mode="promise_in_bounds")


def pack_kernel(
    depth, moment, bed, send, back, kinds_far, trace_far, mortar_far, levels_far,
    state, traces, wide_a, narrow_b, narrow_a, wide_b, kinds, trace_src, mortar_src, levels,
    *rest
):
    out_refs, scratch = rest[:5], rest[5:7]
    send_list, back_list, sems, list_sems = rest[7:]
    list_copies = [
        pltpu.make_async_copy(send, send_list, list_sems.at[0]),
        pltpu.make_async_copy(back, back_list, list_sems.at[1]),
    ]
    for copy in list_copies:
        copy.start()
    copies = []
    table_copies = [
        pltpu.make_async_copy(kinds_far, kinds, list_sems.at[2]),
        pltpu.make_async_copy(trace_far, trace_src, list_sems.at[3]),
        pltpu.make_async_copy(mortar_far, mortar_src, list_sems.at[4]),
        pltpu.make_async_copy(levels_far, levels, list_sems.at[5]),
    ]
    for block in range(BLOCKS):
        lanes = pl.ds(block * LANES, LANES)
        base = block * STATE
        for slot, (source, row, count) in enumerate(
            ((depth, 0, 64), (moment, 64, 128), (bed, 192, 64))
        ):
            copy = pltpu.make_async_copy(
                source.at[:, lanes], state.at[pl.ds(base + row, count)], sems.at[slot, block]
            )
            copy.start()
            copies.append(copy)
    for copy in table_copies:
        copy.start()
    for copy in list_copies:
        copy.wait()
    lane_id = lax.broadcasted_iota(I32, (8, LANES), 1)
    def full(row):
        row = row.reshape(1, row.shape[0])
        return spread(jnp.concatenate([row, jnp.zeros((1, LANES - row.shape[1]), I32)], axis=1))

    send_first = spread(send_list[pl.ds(0, LANES)].reshape(1, LANES))
    send_last = full(send_list[pl.ds(LANES, 16)])
    back_row = full(back_list[...])
    backs = (pltpu.roll(back_row, 48, 1), pltpu.roll(back_row, 64, 1), back_row, back_row)
    index = []
    for way in range(4):
        row = send_first
        if way == 3:
            row = jnp.where(lane_id < 64, send_last, send_first)
        inside = (lane_id >= BACK_AT[way]) & (lane_id < BACK_AT[way] + BACK_CAP[way])
        row = jnp.where(inside, backs[way], row)
        index.append(row - way * ELEMS)
    out = [[jnp.zeros((8, LANES), F32) for _ in range(4)] for _ in range(4)]
    lane = [row & (LANES - 1) for row in index]
    place = [row >> 7 for row in index]
    for block in range(BLOCKS):
        for copy in copies[3 * block : 3 * block + 3]:
            copy.wait()
        for face in range(FACES):
            for comp in range(4):
                piece = state[face_rows(block * STATE + component(face, comp) * 64, face), :]
                if comp == 0:
                    height = piece
                elif comp == 3:
                    piece = piece + height
                traces[pl.ds(trace_row(block, face, comp), 8), :] = piece
    for way in range(4):
        for block in range(BLOCKS):
            here = place[way] == block
            for comp in range(4):
                got = pick(traces[pl.ds(trace_row(block, way, comp), 8), :], lane[way])
                out[way][comp] = got if block == 0 else jnp.where(here, got, out[way][comp])
    wide_even = (lax.axis_index("wide") & 1) == 0
    narrow_even = (lax.axis_index("narrow") & 1) == 0
    for comp in range(4):
        rows = pl.ds(comp * 8, 8)
        wide_a[rows, :] = jnp.where(wide_even, out[1][comp], out[0][comp])
        wide_b[rows, :] = jnp.where(wide_even, out[0][comp], out[1][comp])
        narrow_a[rows, :] = jnp.where(narrow_even, out[3][comp], out[2][comp])
        narrow_b[rows, :] = jnp.where(narrow_even, out[2][comp], out[3][comp])
    for copy in table_copies:
        copy.wait()
    work = block_worker(state, traces, kinds, trace_src, mortar_src, levels, out_refs, scratch)

    work_through(work, 0, blocks_ahead())


def line_terms(height, normal, tangent, bed, marks):
    def accumulate(slot, i, value, minus=False):
        if slot[i] is None:
            slot[i] = -value if minus else value
        else:
            slot[i] = slot[i] - value if minus else slot[i] + value

    slope = [None] * 8
    for i in range(8):
        for k in range(i + 1, 8):
            bump = float(SKEW[i, k]) * (bed[k] - bed[i])
            accumulate(slope, i, bump)
            accumulate(slope, k, bump)
        yield
    square = [2.0 * (h * h) for h in height]
    mass = [None] * 8
    along = [(4.0 * height[i]) * slope[i] for i in range(8)]
    cross = [None] * 8
    for i in range(8):
        for k in range(i + 1, 8):
            q = float(SKEW[i, k])
            un = normal[i] + normal[k]
            if marks:
                un = un + marks.pop(0)
            first = (q * (height[i] + height[k])) * un
            second = first * un + q * (square[i] + square[k])
            third = first * (tangent[i] + tangent[k])
            for slot, value in ((mass, first), (along, second), (cross, third)):
                accumulate(slot, i, value)
                accumulate(slot, k, value, True)
            yield
    out = []
    for i in range(8):
        scale = STEP / WEIGHTS[i]
        out.append(
            (float(0.5 * scale) * mass[i], float(0.25 * scale) * along[i], float(0.25 * scale) * cross[i])
        )
    return out


def volume_of(state, moved, speeds, base, into, metric, marks):
    def rows(comp, j, across):
        if across:
            return pl.ds(comp * 64 + j, 8, stride=8)
        return pl.ds(comp * 64 + j * 8, 8)

    def at(start, window):
        return pl.ds(start + window.start, window.size, window.stride)

    height = [state[at(base, rows(0, j, False)), :] for j in range(8)]
    bed = [state[at(base, rows(3, j, False)), :] for j in range(8)]
    vel_x, vel_y = [], []
    for j in range(8):
        inverse = 1.0 / height[j]
        vel_x.append(state[at(base, rows(1, j, False)), :] * inverse)
        vel_y.append(state[at(base, rows(2, j, False)), :] * inverse)
        speeds[rows(0, j, False), :] = vel_x[j]
        speeds[rows(1, j, False), :] = vel_y[j]
    terms = yield from line_terms(height, vel_x, vel_y, bed, marks)
    for i in range(8):
        for comp, value in enumerate(terms[i]):
            moved[at(into, rows(comp, i, False)), :] = (
                state[at(base, rows(comp, i, False)), :] - metric * value
            )
    height = [state[at(base, rows(0, j, True)), :] for j in range(8)]
    bed = [state[at(base, rows(3, j, True)), :] for j in range(8)]
    vel_x = [speeds[rows(0, j, True), :] for j in range(8)]
    vel_y = [speeds[rows(1, j, True), :] for j in range(8)]
    terms = yield from line_terms(height, vel_y, vel_x, bed, marks)
    for j in range(8):
        mass, along, cross = terms[j]
        for comp, value in enumerate((mass, cross, along)):
            window = at(into, rows(comp, j, True))
            moved[window, :] = moved[window, :] - metric * value


def gather_of(traces, found, picks, block, tree, marks):
    for face in range(FACES):
        own = range(tree * TREE_BLOCKS, (tree + 1) * TREE_BLOCKS)
        reach = range(BLOCKS) if face == 3 - tree else own
        for turn in range(2):
            lane = spread(picks[pl.ds(turn * 8 + face, 1), :])
            place = spread(picks[pl.ds(turn * 8 + 4 + face, 1), :])
            total = [None] * 4
            for other in reach:
                here = place == other
                for comp in range(4):
                    got = pick(traces[pl.ds(trace_row(other, face ^ 1, comp), 8), :], lane)
                    total[comp] = got if total[comp] is None else jnp.where(here, got, total[comp])
                yield
            for comp in range(4):
                row = ((turn * BLOCKS + block) * 4 + face) * 32 + comp * 8
                found[rows_of(row, 8), :] = total[comp]
            marks.append(0.0 * total[3])


def interleave(*works):
    works = list(works)
    while works:
        for work in list(works):
            if next(work, works) is works:
                works.remove(work)


def block_worker(state, traces, kinds, trace_src, mortar_src, levels, out, scratch):
    moved, found, codes, rows_kind, rows_factor = out
    speeds, picks = scratch
    face_id = lax.broadcasted_iota(I32, (4, LANES), 0)

    def by_face(values):
        total = jnp.full((4, LANES), values[3], I32)
        for face in range(3):
            total = jnp.where(face_id == face, values[face], total)
        return total

    home = by_face([-(face ^ 1) * ELEMS for face in range(FACES)])
    recv_shift = by_face([RECV_LANE[f] - RECV_OFF[f] - LOCAL for f in range(FACES)])
    retn_shift = by_face([RETN_LANE[f] - RETN_OFF[f] - LOCAL for f in range(FACES)])

    def work(block, tree):
        lanes = lanes_of(block)
        base = pl.multiple_of(block * STATE, STATE)
        into = pl.multiple_of(block * MOVED, MOVED)
        level_row = (levels[lanes].reshape(1, LANES) + 1).astype(F32)
        kind = kinds[:, lanes]
        coarse = kind == 3
        first = jnp.where(coarse, mortar_src[0, :, lanes], trace_src[:, lanes])
        second = mortar_src[1, :, lanes]
        four = pl.ds(pl.multiple_of(block * 4, 4), 4)
        for turn, (index, shift) in enumerate(
            ((first, jnp.where(coarse, retn_shift, recv_shift)), (second, retn_shift))
        ):
            far = index >= LOCAL
            index = index + jnp.where(far, shift, home)
            lane = index & (LANES - 1)
            picks[pl.ds(turn * 8, 4), :] = lane
            picks[pl.ds(turn * 8 + 4, 4), :] = jnp.where(far, BLOCKS, index >> 7)
            codes[turn, four, :] = jnp.where(far, lane + LANES, lane)
        rows_kind[four, :] = kind
        rows_factor[four, :] = jnp.broadcast_to(level_row * float(0.5 * LIFT * STEP), (4, LANES))
        marks = []
        interleave(
            gather_of(traces, found, picks, block, tree, marks),
            volume_of(state, moved, speeds, base, into, spread(level_row), marks),
        )

    return work


def work_through(work, start, stop):
    for tree in range(2):

        def step(block, carry, tree=tree):
            work(block, tree)
            return carry

        low, high = tree * TREE_BLOCKS, (tree + 1) * TREE_BLOCKS
        lax.fori_loop(jnp.maximum(start, low), jnp.minimum(stop, high), step, 0)


def blocks_ahead():
    wide, narrow = lax.axis_index("wide"), lax.axis_index("narrow")
    x, z, core = wide >> 3, (wide >> 1) & 3, wide & 1

    def one_of(at, values):
        total = jnp.int32(values[3])
        for i in range(3):
            total = jnp.where(at == i, jnp.int32(values[i]), total)
        return total

    lead = AHEAD - one_of(narrow, (0, 0, 28, 35)) - one_of(x, (0, 10, 12, 14)) - one_of(z, (0, 10, 22, 26))
    ahead = jnp.clip((lead + 5 * core) // PER_BLOCK, 0, TREE_BLOCKS)
    return ahead + jnp.where((wide == 0) & (narrow < 2), FIRST_MORE, 0)


def interior_kernel(
    state, traces, kinds, trace_src, mortar_src, levels, *rest
):
    out, scratch = rest[5:10], rest[10:]
    work = block_worker(state, traces, kinds, trace_src, mortar_src, levels, out, scratch)

    work_through(work, blocks_ahead(), BLOCKS)


def numeric_flux(left, right, sign):
    inv_l, inv_r = 1.0 / left[0], 1.0 / right[0]
    un_l, un_r = left[1] * inv_l, right[1] * inv_r
    un = un_l + un_r
    ut = left[2] * inv_l + right[2] * inv_r
    speed = jnp.maximum(
        jnp.abs(un_l) + left[0] * lax.rsqrt(left[0]), jnp.abs(un_r) + right[0] * lax.rsqrt(right[0])
    )
    first = (sign * (left[0] + right[0])) * un
    middle = 0.5 * first
    second = middle * un + sign * (left[0] * left[0] + right[0] * right[0])
    third = middle * ut
    return (
        first - speed * (right[3] - left[3]),
        second - speed * (right[1] - left[1]),
        third - speed * (right[2] - left[2]),
    )


def weighted(coefficients, values):
    total = None
    for coefficient, value in zip(coefficients, values):
        if abs(coefficient) > 1e-12:
            term = float(coefficient) * value
            total = term if total is None else total + term
    return total


def weighted(coefficients, values):
    total = None
    for coefficient, value in zip(coefficients, values):
        term = float(coefficient) * value
        total = term if total is None else total + term
    return total


def surface_kernel(
    moved_in, traces, found, codes, rows_kind, rows_factor, got_wa, got_nb, got_na, got_wb,
    new_depth, new_moment, moved, came, near_a, near_b, changes, sems
):
    del moved_in
    wide_even = (lax.axis_index("wide") & 1) == 0
    narrow_even = (lax.axis_index("narrow") & 1) == 0
    for comp in range(4):
        rows = pl.ds(comp * 8, 8)
        wide = got_wa[rows, :], got_wb[rows, :]
        narrow = got_na[rows, :], got_nb[rows, :]
        came[pl.ds(comp * 8, 8), :] = jnp.where(wide_even, wide[1], wide[0])
        came[pl.ds(32 + comp * 8, 8), :] = jnp.where(wide_even, wide[0], wide[1])
        came[pl.ds(64 + comp * 8, 8), :] = jnp.where(narrow_even, narrow[1], narrow[0])
        came[pl.ds(96 + comp * 8, 8), :] = jnp.where(narrow_even, narrow[0], narrow[1])
    row_id = lax.broadcasted_iota(I32, (8, LANES), 0)
    normal_half = jnp.where((row_id & 1) == 1, 0.5, -0.5).astype(F32)

    def copies(block):
        lanes = lanes_of(block)
        row = pl.multiple_of(block * MOVED, MOVED)
        return (
            pltpu.make_async_copy(moved.at[pl.ds(row, 64)], new_depth.at[:, lanes], sems.at[0, block]),
            pltpu.make_async_copy(
                moved.at[pl.ds(row + 64, 128)], new_moment.at[:, lanes], sems.at[1, block]
            ),
        )

    def fetch(group, near, marks):
        for face in range(FACES):
            for turn in range(2):
                for half in range(2):
                    spot = half * 4 + face
                    code = spread(codes[turn, pl.ds(group * 8 + spot, 1), :])
                    far = code >= LANES
                    lane = code & (LANES - 1)
                    for comp in range(4):
                        row = ((turn * BLOCKS + group * 2 + half) * 4 + face) * 32 + comp * 8
                        there = pick(came[pl.ds(face * 32 + comp * 8, 8), :], lane)
                        near[pl.ds((turn * 4 + comp) * 64 + spot * 8, 8), :] = jnp.where(
                            far, there, found[rows_of(row, 8), :]
                        )
                    marks.append(0.0 * there)
                    yield

    def settle(group, near, marks):
        eight = pl.ds(pl.multiple_of(group * 8, 8), 8)
        kind = rows_kind[eight, :]
        factor = rows_factor[eight, :]
        coarse, lower, upper = kind == 3, kind == 1, kind == 2
        left, right, high = [], [], []
        for comp in range(4):
            own = [
                traces[pl.ds(group * 256 + comp * 64 + node, 8, stride=8), :] for node in range(8)
            ]
            other = [near[pl.ds(comp * 64 + node, 8, stride=8), :] for node in range(8)]
            blend = [jnp.where(coarse, own[n], other[n]) for n in range(8)]
            even = [blend[b] + blend[7 - b] for b in range(4)]
            odd = [blend[b] - blend[7 - b] for b in range(4)]
            low_of, high_of = [None] * 8, [None] * 8
            for a in range(8):
                one, two = weighted(FOLD_EVEN[a], even), weighted(FOLD_ODD[a], odd)
                if a == 0:
                    low_of[0], high_of[7] = blend[0], blend[7]
                elif two is None:
                    low_of[a] = high_of[7 - a] = one
                else:
                    low_of[a], high_of[7 - a] = one + two, one - two
                if a % 2:
                    yield
            left.append([jnp.where(coarse, low_of[n], own[n]) for n in range(8)])
            right.append(
                [jnp.where(lower, low_of[n], jnp.where(upper, high_of[n], other[n])) for n in range(8)]
            )
            high.append(high_of)
        one, two = [], []
        for node in range(8):
            above = [near[pl.ds((4 + comp) * 64 + node, 8, stride=8), :] for comp in range(4)]
            sign = normal_half
            for _ in range(min(2, len(marks))):
                sign = sign + marks.pop(0)
            one.append(numeric_flux([v[node] for v in left], [v[node] for v in right], sign))
            two.append(numeric_flux([v[node] for v in high], above, sign))
            yield
        for comp in range(3):
            total = [one[b][comp] + two[7 - b][comp] for b in range(8)]
            differ = [one[b][comp] - two[7 - b][comp] for b in range(8)]
            for a in range(4):
                same, anti = weighted(JOIN_SUM[a], total), weighted(JOIN_DIFF[a], differ)
                for node, joined in ((a, same + anti), (7 - a, same - anti)):
                    changes[pl.ds(comp * 64 + node, 8, stride=8), :] = factor * jnp.where(
                        coarse, joined, one[node][comp]
                    )
        for half in range(2):
            into = pl.multiple_of((group * 2 + half) * MOVED, MOVED)
            for face in range(FACES):
                for comp in range(3):
                    rows = face_rows(into + component(face, comp) * 64, face)
                    moved[rows, :] = (
                        moved[rows, :] - changes[pl.ds(comp * 64 + (half * 4 + face) * 8, 8), :]
                    )
            for copy in copies(group * 2 + half):
                copy.start()

    def both(next_group, into, group, held):
        marks = []
        interleave(fetch(next_group, into, marks), settle(group, held, marks))

    def body(step, carry):
        both(2 * step + 1, near_b, 2 * step, near_a)
        both(2 * step + 2, near_a, 2 * step + 1, near_b)
        return carry

    interleave(fetch(0, near_a, []))
    lax.fori_loop(0, GROUPS // 2, body, 0)
    interleave(settle(GROUPS - 1, near_a, []))

    def finish(block, carry):
        for copy in copies(block):
            copy.wait()
        return carry

    lax.fori_loop(0, BLOCKS, finish, 0)


VM = pl.BlockSpec(memory_space=pltpu.VMEM)
FAR = pl.BlockSpec(memory_space=pltpu.HBM)
ANY = pl.BlockSpec(memory_space=pl.ANY)
PARAMS = pltpu.CompilerParams(vmem_limit_bytes=24 * 1024 * 1024)


def swap(block, axis, phase):
    size = lax.axis_size(axis)
    route = [(i, (((i + phase) ^ 1) - phase) % size) for i in range(size)]
    return lax.ppermute(block, axis, route)


def placed(memory, *arrays):
    return [pltpu.with_memory_space_constraint(array, memory) for array in arrays]


def on_device(depth, momentum, bed, levels, kinds, send, trace_src, back, mortar_src):
    depth = depth.reshape(64, ELEMS)
    momentum = momentum.reshape(128, ELEMS)
    bed = bed.reshape(64, ELEMS)
    message = pltpu.VMEM((32, LANES), F32)
    tables = (
        pltpu.VMEM((4, ELEMS), I32),
        pltpu.VMEM((4, ELEMS), I32),
        pltpu.VMEM((2, 4, ELEMS), I32),
        pltpu.VMEM((ELEMS,), I32),
    )
    done = (
        pltpu.VMEM((BLOCKS * MOVED, LANES), F32),
        pltpu.VMEM((2 * BLOCKS * 128, LANES), F32),
        pltpu.VMEM((2, 4 * BLOCKS, LANES), I32),
        pltpu.VMEM((4 * BLOCKS, LANES), I32),
        pltpu.VMEM((4 * BLOCKS, LANES), F32),
    )
    held = pltpu.VMEM((BLOCKS * STATE, LANES), F32), pltpu.VMEM((BLOCKS * TRACE, LANES), F32)
    work_space = [pltpu.VMEM((128, LANES), F32), pltpu.VMEM((16, LANES), I32)]
    packed = pl.pallas_call(
        pack_kernel,
        out_shape=held + (message,) * 4 + tables + done,
        in_specs=[FAR] * 9,
        out_specs=[VM] * 15,
        scratch_shapes=work_space
        + [
            pltpu.VMEM((144,), I32),
            pltpu.VMEM((96,), I32),
            pltpu.SemaphoreType.DMA((3, BLOCKS)),
            pltpu.SemaphoreType.DMA((6,)),
        ],
        compiler_params=PARAMS,
        name="pack",
    )(*placed(pltpu.HBM, depth, momentum, bed, send, back, kinds, trace_src, mortar_src, levels))
    state, traces = packed[:2]
    wide_a, narrow_b, narrow_a, wide_b = packed[2:6]
    got_wb = swap(wide_b, "wide", 1)
    got_na = swap(narrow_a, "narrow", 0)
    got_nb = swap(narrow_b, "narrow", 1)
    got_wa = swap(wide_a, "wide", 0)
    moved, found, codes, rows_kind, rows_factor = pl.pallas_call(
        interior_kernel,
        out_shape=done,
        in_specs=[VM] * 11,
        out_specs=[VM] * 5,
        input_output_aliases={6 + i: i for i in range(5)},
        scratch_shapes=work_space,
        compiler_params=PARAMS,
        name="interior",
        cost_estimate=pl.CostEstimate(flops=20_000_000, bytes_accessed=2_000_000, transcendentals=0),
    )(*placed(pltpu.VMEM, state, traces, *packed[6:15]))
    new_depth, new_moment, _ = pl.pallas_call(
        surface_kernel,
        out_shape=(
            jax.ShapeDtypeStruct((64, ELEMS), F32),
            jax.ShapeDtypeStruct((128, ELEMS), F32),
            pltpu.VMEM((BLOCKS * MOVED, LANES), F32),
        ),
        in_specs=[VM] * 10,
        out_specs=[ANY, ANY, VM],
        input_output_aliases={0: 2},
        scratch_shapes=[
            pltpu.VMEM((128, LANES), F32),
            pltpu.VMEM((512, LANES), F32),
            pltpu.VMEM((512, LANES), F32),
            pltpu.VMEM((192, LANES), F32),
            pltpu.SemaphoreType.DMA((2, BLOCKS)),
        ],
        compiler_params=PARAMS,
        name="surface",
    )(
        *placed(
            pltpu.VMEM, moved, traces, found, codes, rows_kind, rows_factor, got_wa, got_nb, got_na, got_wb
        )
    )
    return new_depth.reshape(8, 8, ELEMS), new_moment.reshape(2, 8, 8, ELEMS)


def solution(mesh):
    both = ("wide", "narrow")
    placed = (
        P(None, None, both),
        P(None, None, None, both),
        P(None, None, both),
        P(both),
        P(None, both),
        P(both),
        P(None, both),
        P(both),
        P(None, None, both),
    )
    return jax.shard_map(
        on_device,
        mesh=mesh,
        in_specs=placed,
        out_specs=(P(None, None, both), P(None, None, None, both)),
        check_vma=False,
    )
```
